256 devices in a mesh: dom: 32 (over z, x), orb: 8 (over y, core).
Axes of the slice: x: 4, y: 4, z: 8, core: 2. Of those that a mesh axis runs over, the one named last changes fastest.
Arguments:
- orbitals: float32 [16, 384, 64, 128], P('orb', 'dom'), may hold values from -400 to 400
- potential: float32 [384, 64, 128], P('dom'), may hold values from -8 to 8
Outputs:
- filtered_basis: float32 [16, 384, 64, 128], P('orb', 'dom')
The draws below stay inside these ranges and needn't reach their ends.
All inputs are finite; a program needn't handle non-finite values.
Results may differ from the reference program's by a relative error of at most 0.0003.
Values sent between devices are 32-bit elements; how exact they have to be, the bound alone decides.
A program may use at most 64 MiB of HBM per device.

```python
import math
import jax
import jax.numpy as jnp
from jax import lax

ORBITALS = 16
NY = 64
NZ = 128
NX = 384


def draw_orbitals(key, part):
    key_base, key_noise, key_scale = jax.random.split(jax.random.fold_in(key, 7), 3)
    scales = jnp.exp(jax.random.uniform(key_scale, (ORBITALS, 1, 1, 1), jnp.float32, 0.0, math.log(10.0)))
    along_x = jnp.arange(NX, dtype=jnp.float32) / max(NX - 1, 1)
    along_y = jnp.arange(NY, dtype=jnp.float32) / max(NY - 1, 1)
    base = jnp.clip(jax.random.normal(key_base, (NX, NY, NZ), jnp.float32), -5.5, 5.5)
    noise = jnp.clip(jax.random.normal(key_noise, (ORBITALS, NX, NY, NZ), jnp.float32), -5.5, 5.5)
    share = 16.0
    envelope = jnp.sqrt((1.0 + 2.0 * along_x)[:, None, None] * (1.0 + 2.0 * along_y)[None, :, None])
    return (scales * envelope[None] * (base[None] + noise / share)).astype(jnp.float32)


def shard_levels(stream_key, shape, shards, smallest, high):
    gain, own = 1.0, jax.random.fold_in(stream_key, 6)
    for dim, blocks in shards:
        steps = jnp.exp(jax.random.uniform(jax.random.fold_in(own, dim), (blocks,), jnp.float32, smallest / len(shards), high / len(shards)))
        gain = gain * jnp.repeat(steps, shape[dim] // blocks).reshape([-1 if axis == dim else 1 for axis in range(len(shape))])
    return gain


def setup_inputs(seed: int = 0) -> dict:
    key_list = jax.random.split(jax.random.key(seed), 3)
    orbitals = draw_orbitals(jax.random.fold_in(key_list[2], 71), 0)
    potential = jnp.clip(jax.random.uniform(key_list[1], (NX, NY, NZ), jnp.float32, -8.0, 8.0) * shard_levels(key_list[1], (NX, NY, NZ), ((0, 32),), -0.4, 0.0), -8.0, 8.0)
    return dict(orbitals=orbitals, potential=potential)


coefficients = (-49.0 / 18.0, 1.5, -0.15, 1.0 / 90.0)
spacing = 0.5
filter_centre = 23.0
filter_half = 23.0

def hamiltonian(field, potential):
    laplace = 3.0 * coefficients[0] * field
    for offset in range(1, 4):
        for axis_number in range(3):
            laplace = laplace + coefficients[offset] * (jnp.roll(field, offset, axis_number) + jnp.roll(field, -offset, axis_number))
    return -0.5 / (spacing * spacing) * laplace + potential * field

def filtered(field, potential):
    first = (hamiltonian(field, potential) - filter_centre * field) / filter_half
    second = 2.0 * (hamiltonian(first, potential) - filter_centre * first) / filter_half - field
    third = 2.0 * (hamiltonian(second, potential) - filter_centre * second) / filter_half - first
    return third

def orthonormal(block, cell_total):
    gram = jnp.dot(block.astype(jnp.float32), block.T.astype(jnp.float32), precision=lax.Precision.HIGHEST, preferred_element_type=jnp.float32) / cell_total
    lower = jnp.linalg.cholesky(gram)
    return lax.linalg.triangular_solve(lower, block, left_side=True, lower=True)

def reference(orbitals, potential):

    def one_orbital(field):
        return filtered(field, potential)
    result = lax.map(one_orbital, orbitals)
    flat = result.reshape(ORBITALS, -1)
    cell_total = NX * NY * NZ
    basis = orthonormal(orthonormal(flat, cell_total), cell_total)
    return basis.reshape(result.shape)
```

```python
import functools

import jax
import jax.numpy as jnp
from jax import lax
from jax.experimental import pallas as pl
from jax.experimental.pallas import tpu as pltpu
from jax.sharding import PartitionSpec as P

MESH = pl.DeviceIdType.MESH
F32 = jnp.float32
BF16 = jnp.bfloat16
coefficients = (-49.0 / 18.0, 1.5, -0.15, 1.0 / 90.0)
spacing = 0.5
filter_centre = 23.0
filter_half = 23.0
kinetic = -0.5 / (spacing * spacing) / filter_half
STEP = tuple(kinetic * c for c in coefficients)
DIAGONAL = 3.0 * STEP[0] - filter_centre / filter_half
PAD = 8


def split3(x):
    hi = x.astype(BF16)
    rest = x - hi.astype(F32)
    mid = rest.astype(BF16)
    low = (rest - mid.astype(F32)).astype(BF16)
    return hi, mid, low


def eliminate(gram, n):
    rows = lax.broadcasted_iota(jnp.int32, (n, 128), 0)
    lanes = lax.broadcasted_iota(jnp.int32, (n, 128), 1)
    work = jnp.where(lanes < n, gram, 0.0) + jnp.where(lanes == rows + n, 1.0, 0.0)
    for j in range(n - 1):
        column = jnp.broadcast_to(work[:, j : j + 1], (n, 128))
        pivot = jnp.broadcast_to(column[j : j + 1, :], (n, 128))
        row = jnp.broadcast_to(work[j : j + 1, :], (n, 128))
        factor = jnp.where(rows > j, column / pivot, 0.0)
        work = work - factor * row
    diagonal = jnp.sum(jnp.where(lanes == rows, work, 0.0), axis=1, keepdims=True)
    scaled = work / jnp.sqrt(jnp.broadcast_to(diagonal, (n, 128)))
    return jnp.where(lanes < n, pltpu.roll(scaled, 128 - n, 1), 0.0)


def kernel(
    sizes,
    orb_ref,
    pot_ref,
    out_ref,
    e0,
    e1,
    e2,
    diag,
    third,
    grouped,
    split_x,
    split_b,
    back,
    gram_orb,
    gram_dom,
    load_sem,
    halo_send,
    halo_recv,
    fwd_send,
    fwd_recv,
    fwd_own,
    gram_send,
    gram_recv,
    bck_send,
    bck_recv,
    bck_own,
):
    doms, orbs, own, layers, ny, nz, cells = sizes
    n = own * orbs
    chunk = ny // orbs
    half = layers - 6
    d = lax.axis_index("dom")
    o = lax.axis_index("orb")
    left = lax.rem(d + doms - 1, doms)
    right = lax.rem(d + 1, doms)

    barrier = pltpu.get_barrier_semaphore()

    @pl.loop(1, orbs)
    def _(p):
        pl.semaphore_signal(
            barrier, inc=1, device_id={"orb": lax.rem(o + p, orbs)}, device_id_type=MESH
        )

    @pl.loop(1, doms)
    def _(p):
        pl.semaphore_signal(
            barrier, inc=1, device_id={"dom": lax.rem(d + p, doms)}, device_id_type=MESH
        )

    loads = [pltpu.make_async_copy(pot_ref, diag, load_sem.at[0])]
    for a in range(own):
        loads.append(
            pltpu.make_async_copy(
                orb_ref.at[a], e0.at[a, pl.ds(3, layers), pl.ds(PAD, ny)], load_sem.at[1 + 3 * a]
            )
        )
        loads.append(
            pltpu.make_async_copy(
                orb_ref.at[a, :, pl.ds(ny - PAD, PAD)],
                e0.at[a, pl.ds(3, layers), pl.ds(0, PAD)],
                load_sem.at[2 + 3 * a],
            )
        )
        loads.append(
            pltpu.make_async_copy(
                orb_ref.at[a, :, pl.ds(0, PAD)],
                e0.at[a, pl.ds(3, layers), pl.ds(PAD + ny, PAD)],
                load_sem.at[3 + 3 * a],
            )
        )
    for copy in loads:
        copy.start()

    pl.semaphore_wait(barrier, orbs - 1 + doms - 1)

    fields = (e0, e1, e2)

    def halo(stage, a):
        dst = fields[stage]
        rows = pl.ds(PAD, ny)
        if stage == 0:
            low_src, high_src = orb_ref.at[a, pl.ds(0, 3)], orb_ref.at[a, pl.ds(layers - 3, 3)]
        else:
            low_src = dst.at[a, pl.ds(3, 3), rows]
            high_src = dst.at[a, pl.ds(layers, 3), rows]
        out = []
        for side, (src, at, to) in enumerate(((high_src, 0, right), (low_src, layers + 3, left))):
            out.append(
                pltpu.make_async_remote_copy(
                    src_ref=src,
                    dst_ref=dst.at[a, pl.ds(at, 3), rows],
                    send_sem=halo_send.at[stage, a, side],
                    recv_sem=halo_recv.at[stage, a, side],
                    device_id={"dom": to},
                    device_id_type=MESH,
                )
            )
        return out

    halos = [[halo(stage, a) for a in range(own)] for stage in range(3)]

    def apply_layer(stage, a, layer, slot):
        src = fields[stage]
        rows = pl.ds(PAD, ny)
        centre = src[a, layer + 3, rows, :]
        result = diag[layer] * centre
        for k in range(1, 4):
            near = src[a, layer + 3 + k, rows, :] + src[a, layer + 3 - k, rows, :]
            near = near + (
                src[a, layer + 3, pl.ds(PAD + k, ny), :] + src[a, layer + 3, pl.ds(PAD - k, ny), :]
            )
            near = near + (pltpu.roll(centre, k, 1) + pltpu.roll(centre, nz - k, 1))
            result = result + STEP[k] * near
        if stage > 0:
            result = 2.0 * result - fields[stage - 1][a, layer + 3, rows, :]
        if stage < 2:
            dst = fields[stage + 1]
            dst[a, layer + 3, rows, :] = result
            dst[a, layer + 3, pl.ds(0, PAD), :] = result[ny - PAD :, :]
            dst[a, layer + 3, pl.ds(PAD + ny, PAD), :] = result[:PAD, :]
        else:
            third[:, a, slot] = result.reshape(orbs, chunk, nz)

    def inner(stage, a):
        @pl.loop(0, half)
        def _(i):
            apply_layer(stage, a, i + 3, i)

    def outer(stage, a):
        @pl.loop(half, layers)
        def _(i):
            apply_layer(stage, a, lax.rem(i + 3, layers), i)

    def to_cells(a, part):
        at, count = (0, half) if part == 0 else (half, 6)

        @pl.loop(1, orbs)
        def _(p):
            to = lax.rem(o + p, orbs)
            pltpu.make_async_remote_copy(
                src_ref=third.at[to, a, pl.ds(at, count)],
                dst_ref=grouped.at[own * o + a, pl.ds(at, count)],
                send_sem=fwd_send.at[a, part],
                recv_sem=fwd_recv.at[a, part],
                device_id={"orb": to},
                device_id_type=MESH,
            ).start()

        pltpu.make_async_copy(
            third.at[o, a, pl.ds(at, count)],
            grouped.at[own * o + a, pl.ds(at, count)],
            fwd_own.at[a, part],
        ).start()

    def wait_cells(a, part):
        at, count = (0, half) if part == 0 else (half, 6)
        block = grouped.at[pl.ds(0, orbs - 1), pl.ds(at, count)]
        pltpu.make_async_copy(block, block, fwd_send.at[a, part]).wait()
        pltpu.make_async_copy(block, block, fwd_recv.at[a, part]).wait()
        single = grouped.at[0, pl.ds(at, count)]
        pltpu.make_async_copy(single, single, fwd_own.at[a, part]).wait()

    for a in range(own):
        for copy in halos[0][a]:
            copy.start()
    for copy in loads:
        copy.wait()

    @pl.loop(0, layers)
    def _(i):
        diag[i] = diag[i] * (1.0 / filter_half) + DIAGONAL

    for a in range(own):
        inner(0, a)
    for stage in range(3):
        for a in range(own):
            for copy in halos[stage][a]:
                copy.wait()
            outer(stage, a)
            if stage < 2:
                for copy in halos[stage + 1][a]:
                    copy.start()
                inner(stage + 1, a)
                if stage == 1:
                    to_cells(a, 0)
            else:
                to_cells(a, 1)

    flat = grouped.reshape(n * layers * chunk, nz)
    flat_back = back.reshape(n * layers * chunk, nz)
    stride = layers * chunk

    def split_slots(begin, end):
        @pl.loop(begin, end)
        def _(slot):
            for r in range(chunk):
                row = slot * chunk + r
                x = flat[pl.ds(row, n, stride=stride), :]
                lanes = pl.ds(pl.multiple_of(row * nz, nz), nz)
                for part, value in enumerate(split3(x)):
                    split_x[pl.ds(part * n, n), lanes] = value

    def gram_of(split, begin, end):
        x = split[:, begin * chunk * nz : end * chunk * nz]
        return lax.dot_general(x, x, (((1,), (1,)), ((), ())), preferred_element_type=F32)

    lane = lax.broadcasted_iota(jnp.int32, (8, 128), 1)

    def total(full, step):
        rows = full[0:n] + full[n : 2 * n] + full[2 * n : 3 * n]
        wide = jnp.concatenate([rows, jnp.zeros((n, 128 - 3 * n), F32)], axis=1)
        wide = wide + pltpu.roll(wide, 128 - n, 1) + pltpu.roll(wide, 128 - 2 * n, 1)
        packed = jnp.where(lane < n, wide[:8], pltpu.roll(wide[8:], n, 1))
        for axis, count, me, buf in (("orb", orbs, o, gram_orb), ("dom", doms, d, gram_dom)):
            which = 0 if axis == "orb" else 1
            buf[step, me] = packed

            @pl.loop(1, count)
            def _(p):
                pltpu.make_async_remote_copy(
                    src_ref=buf.at[step, me],
                    dst_ref=buf.at[step, me],
                    send_sem=gram_send.at[step, which],
                    recv_sem=gram_recv.at[step, which],
                    device_id={axis: lax.rem(me + p, count)},
                    device_id_type=MESH,
                ).start()

            block = buf.at[step, pl.ds(0, count - 1)]
            pltpu.make_async_copy(block, block, gram_send.at[step, which]).wait()
            pltpu.make_async_copy(block, block, gram_recv.at[step, which]).wait()
            packed = jnp.sum(buf[step], axis=0)
        packed = packed * (1.0 / cells)
        return jnp.concatenate([packed, pltpu.roll(packed, 128 - n, 1)], axis=0)

    def stacked(inverse):
        wide = inverse + pltpu.roll(inverse, n, 1) + pltpu.roll(inverse, 2 * n, 1)
        return jnp.concatenate(split3(wide), axis=0)[:, : 3 * n]

    def applied(weights, split, lanes):
        full = jnp.dot(weights, split[:, lanes], preferred_element_type=F32)
        return full[0:n] + (full[n : 2 * n] + full[2 * n : 3 * n])

    for a in range(own):
        wait_cells(a, 0)
    split_slots(0, half)
    full = gram_of(split_x, 0, half)
    for a in range(own):
        wait_cells(a, 1)
    split_slots(half, layers)
    full = full + gram_of(split_x, half, layers)

    weights_one = stacked(eliminate(total(full, 0), n))

    @pl.loop(0, layers)
    def _(slot):
        lanes = pl.ds(pl.multiple_of(slot * chunk * nz, chunk * nz), chunk * nz)
        for part, value in enumerate(split3(applied(weights_one, split_x, lanes))):
            split_b[pl.ds(part * n, n), lanes] = value

    weights_two = stacked(eliminate(total(gram_of(split_b, 0, layers), 1), n))

    def send_back(part, at, count, layer):
        @pl.loop(1, orbs)
        def _(p):
            to = lax.rem(o + p, orbs)
            pltpu.make_async_remote_copy(
                src_ref=back.at[pl.ds(own * to, own), pl.ds(at, count)],
                dst_ref=out_ref.at[:, pl.ds(layer, count), pl.ds(chunk * o, chunk)],
                send_sem=bck_send.at[part],
                recv_sem=bck_recv.at[part],
                device_id={"orb": to},
                device_id_type=MESH,
            ).start()

        pltpu.make_async_copy(
            back.at[pl.ds(own * o, own), pl.ds(at, count)],
            out_ref.at[:, pl.ds(layer, count), pl.ds(chunk * o, chunk)],
            bck_own.at[part],
        ).start()

    parts = ((0, half, 3), (half, 3, half + 3), (half + 3, 3, 0))
    for part, (at, count, layer) in enumerate(parts):

        @pl.loop(at, at + count)
        def _(slot):
            lanes = pl.ds(pl.multiple_of(slot * chunk * nz, chunk * nz), chunk * nz)
            y = applied(weights_two, split_b, lanes)
            for r in range(chunk):
                flat_back[pl.ds(slot * chunk + r, n, stride=stride), :] = y[:, r * nz : (r + 1) * nz]

        send_back(part, at, count, layer)
    for part, (at, count, layer) in enumerate(parts):
        block = back.at[pl.ds(0, own * (orbs - 1)), pl.ds(at, count)]
        pltpu.make_async_copy(block, block, bck_send.at[part]).wait()
        pltpu.make_async_copy(block, block, bck_recv.at[part]).wait()
        single = back.at[pl.ds(0, own), pl.ds(at, count)]
        pltpu.make_async_copy(single, single, bck_own.at[part]).wait()


def on_device(orbitals, potential):
    own, layers, ny, nz = orbitals.shape
    doms, orbs = lax.axis_size("dom"), lax.axis_size("orb")
    n = own * orbs
    chunk = ny // orbs
    cells = layers * doms * ny * nz
    width = layers * chunk * nz
    dma = pltpu.SemaphoreType.DMA
    field = pltpu.VMEM((own, layers + 6, ny + 2 * PAD, nz), F32)
    return pl.pallas_call(
        functools.partial(kernel, (doms, orbs, own, layers, ny, nz, cells)),
        out_shape=jax.ShapeDtypeStruct(orbitals.shape, F32),
        in_specs=[pl.BlockSpec(memory_space=pl.ANY)] * 2,
        out_specs=pl.BlockSpec(memory_space=pl.ANY),
        scratch_shapes=[
            field,
            field,
            field,
            pltpu.VMEM((layers, ny, nz), F32),
            pltpu.VMEM((orbs, own, layers, chunk, nz), F32),
            pltpu.VMEM((n, layers, chunk, nz), F32),
            pltpu.VMEM((3 * n, width), BF16),
            pltpu.VMEM((3 * n, width), BF16),
            pltpu.VMEM((n, layers, chunk, nz), F32),
            pltpu.VMEM((2, orbs, 8, 128), F32),
            pltpu.VMEM((2, doms, 8, 128), F32),
            dma((1 + 3 * own,)),
            dma((3, own, 2)),
            dma((3, own, 2)),
            dma((own, 2)),
            dma((own, 2)),
            dma((own, 2)),
            dma((2, 2)),
            dma((2, 2)),
            dma((3,)),
            dma((3,)),
            dma((3,)),
        ],
        compiler_params=pltpu.CompilerParams(
            collective_id=0, has_side_effects=True, vmem_limit_bytes=40 * 1024 * 1024
        ),
        cost_estimate=pl.CostEstimate(flops=100_000_000, bytes_accessed=4_000_000, transcendentals=0),
    )(orbitals, potential)


def solution(mesh):
    return jax.shard_map(
        on_device,
        mesh=mesh,
        in_specs=(P("orb", "dom", None, None), P("dom", None, None)),
        out_specs=P("orb", "dom", None, None),
        check_vma=False,
    )
```

```python
import functools

import jax
import jax.numpy as jnp
from jax import lax
from jax.experimental import pallas as pl
from jax.experimental.pallas import tpu as pltpu
from jax.sharding import PartitionSpec as P

MESH = pl.DeviceIdType.MESH
F32 = jnp.float32
BF16 = jnp.bfloat16
coefficients = (-49.0 / 18.0, 1.5, -0.15, 1.0 / 90.0)
spacing = 0.5
filter_centre = 23.0
filter_half = 23.0
kinetic = -0.5 / (spacing * spacing) / filter_half
STEP = tuple(kinetic * c for c in coefficients)
DIAGONAL = 3.0 * STEP[0] - filter_centre / filter_half
PAD = 8
LIMBS = 4


def split3(x):
    hi = x.astype(BF16)
    rest = x - hi.astype(F32)
    mid = rest.astype(BF16)
    low = (rest - mid.astype(F32)).astype(BF16)
    return hi, mid, low


def anchor_of(largest):
    shift = largest * 2.0**23
    return ((largest + shift) - shift) * (1.25 * 2.0**17)


def limbs(x, anchor):
    out = []
    for part in range(LIMBS):
        place = anchor * 2.0 ** (-8 * part)
        value = (x + place) - place
        x = x - value
        out.append(value.astype(BF16))
    return out


def two_sum(a, b):
    total = a + b
    part = total - a
    return total, (a - (total - part)) + (b - part)


def add_pairs(a, b):
    total, error = two_sum(a[0], b[0])
    return total, error + (a[1] + b[1])


def halves(x):
    wide = x * 4097.0
    high = wide - (wide - x)
    return high, x - high


def lane_of(x, j):
    return jnp.broadcast_to(x[:, j : j + 1], x.shape)


def row_of(x, j):
    return jnp.broadcast_to(x[j : j + 1, :], x.shape)


def product(left, right, n):
    left_high, left_low = halves(left[0])
    right_high, right_low = halves(right[0])
    total, low = None, None
    for k in range(n):
        a, ah, al = lane_of(left[0], k), lane_of(left_high, k), lane_of(left_low, k)
        b, bh, bl = row_of(right[0], k), row_of(right_high, k), row_of(right_low, k)
        value = a * b
        error = ((ah * bh - value) + ah * bl + al * bh) + al * bl
        if right[1] is not None:
            error = error + a * row_of(right[1], k)
        if left[1] is not None:
            error = error + lane_of(left[1], k) * b
        if total is None:
            total, low = value, error
        else:
            total, carry = two_sum(total, value)
            low = low + (carry + error)
    return total, low


def eliminate(gram, n):
    rows = lax.broadcasted_iota(jnp.int32, (n, 128), 0)
    lanes = lax.broadcasted_iota(jnp.int32, (n, 128), 1)
    work = jnp.where(lanes < n, gram, 0.0) + jnp.where(lanes == rows + n, 1.0, 0.0)
    for j in range(n - 1):
        column = lane_of(work, j)
        factor = jnp.where(rows > j, column / row_of(column, j), 0.0)
        work = work - factor * row_of(work, j)
    diagonal = jnp.sum(jnp.where(lanes == rows, work, 0.0), axis=1, keepdims=True)
    scaled = work / jnp.sqrt(jnp.broadcast_to(diagonal, (n, 128)))
    return jnp.where(lanes < n, pltpu.roll(scaled, 128 - n, 1), 0.0)


def combined(gram, cells, n):
    scale = 2.0**-20
    high, low = gram[0] * scale, gram[1] * scale
    rest = 1.0 / (cells * scale)
    inverse_one = eliminate(high * rest, n)
    turned = jnp.transpose(inverse_one)[:n]
    turned = jnp.concatenate([turned, jnp.zeros((n, 128 - n), F32)], axis=1)
    half = product((inverse_one, None), (high, low), n)
    gram_two = product(half, (turned, None), n)
    inverse_two = eliminate((gram_two[0] + gram_two[1]) * rest, n)
    both = lane_of(inverse_two, 0) * row_of(inverse_one, 0)
    for k in range(1, n):
        both = both + lane_of(inverse_two, k) * row_of(inverse_one, k)
    return both


def kernel(
    sizes,
    orb_ref,
    pot_ref,
    out_ref,
    e0,
    e1,
    e2,
    diag,
    third,
    grouped,
    split_x,
    back,
    gram_orb,
    gram_dom,
    load_sem,
    halo_send,
    halo_recv,
    fwd_send,
    fwd_recv,
    fwd_own,
    gram_send,
    gram_recv,
    bck_send,
    bck_recv,
    bck_own,
):
    doms, orbs, own, layers, ny, nz, cells = sizes
    n = own * orbs
    chunk = ny // orbs
    half = layers - 6
    d = lax.axis_index("dom")
    o = lax.axis_index("orb")
    left = lax.rem(d + doms - 1, doms)
    right = lax.rem(d + 1, doms)

    barrier = pltpu.get_barrier_semaphore()

    @pl.loop(1, orbs)
    def _(p):
        pl.semaphore_signal(
            barrier, inc=1, device_id={"orb": lax.rem(o + p, orbs)}, device_id_type=MESH
        )

    @pl.loop(1, doms)
    def _(p):
        pl.semaphore_signal(
            barrier, inc=1, device_id={"dom": lax.rem(d + p, doms)}, device_id_type=MESH
        )

    loads = [pltpu.make_async_copy(pot_ref, diag, load_sem.at[0])]
    for a in range(own):
        loads.append(
            pltpu.make_async_copy(
                orb_ref.at[a], e0.at[a, pl.ds(3, layers), pl.ds(PAD, ny)], load_sem.at[1 + 3 * a]
            )
        )
        loads.append(
            pltpu.make_async_copy(
                orb_ref.at[a, :, pl.ds(ny - PAD, PAD)],
                e0.at[a, pl.ds(3, layers), pl.ds(0, PAD)],
                load_sem.at[2 + 3 * a],
            )
        )
        loads.append(
            pltpu.make_async_copy(
                orb_ref.at[a, :, pl.ds(0, PAD)],
                e0.at[a, pl.ds(3, layers), pl.ds(PAD + ny, PAD)],
                load_sem.at[3 + 3 * a],
            )
        )
    for copy in loads:
        copy.start()

    pl.semaphore_wait(barrier, orbs - 1 + doms - 1)

    fields = (e0, e1, e2)

    def halo(stage, a):
        dst = fields[stage]
        rows = pl.ds(PAD, ny)
        if stage == 0:
            low_src, high_src = orb_ref.at[a, pl.ds(0, 3)], orb_ref.at[a, pl.ds(layers - 3, 3)]
        else:
            low_src = dst.at[a, pl.ds(3, 3), rows]
            high_src = dst.at[a, pl.ds(layers, 3), rows]
        out = []
        for side, (src, at, to) in enumerate(((high_src, 0, right), (low_src, layers + 3, left))):
            out.append(
                pltpu.make_async_remote_copy(
                    src_ref=src,
                    dst_ref=dst.at[a, pl.ds(at, 3), rows],
                    send_sem=halo_send.at[stage, a, side],
                    recv_sem=halo_recv.at[stage, a, side],
                    device_id={"dom": to},
                    device_id_type=MESH,
                )
            )
        return out

    halos = [[halo(stage, a) for a in range(own)] for stage in range(3)]

    def apply_layer(stage, a, layer, slot):
        src = fields[stage]
        rows = pl.ds(PAD, ny)
        centre = src[a, layer + 3, rows, :]
        result = diag[layer] * centre
        for k in range(1, 4):
            near = src[a, layer + 3 + k, rows, :] + src[a, layer + 3 - k, rows, :]
            near = near + (
                src[a, layer + 3, pl.ds(PAD + k, ny), :] + src[a, layer + 3, pl.ds(PAD - k, ny), :]
            )
            near = near + (pltpu.roll(centre, k, 1) + pltpu.roll(centre, nz - k, 1))
            result = result + STEP[k] * near
        if stage > 0:
            result = 2.0 * result - fields[stage - 1][a, layer + 3, rows, :]
        if stage < 2:
            dst = fields[stage + 1]
            dst[a, layer + 3, rows, :] = result
            dst[a, layer + 3, pl.ds(0, PAD), :] = result[ny - PAD :, :]
            dst[a, layer + 3, pl.ds(PAD + ny, PAD), :] = result[:PAD, :]
        else:
            third[:, a, slot] = result.reshape(orbs, chunk, nz)

    def inner(stage, a):
        @pl.loop(0, half, unroll=True)
        def _(i):
            apply_layer(stage, a, i + 3, i)

    def outer(stage, a):
        @pl.loop(half, layers, unroll=True)
        def _(i):
            apply_layer(stage, a, lax.rem(i + 3, layers), i)

    def to_cells(a, part):
        at, count = (0, half) if part == 0 else (half, 6)

        @pl.loop(1, orbs)
        def _(p):
            to = lax.rem(o + p, orbs)
            pltpu.make_async_remote_copy(
                src_ref=third.at[to, a, pl.ds(at, count)],
                dst_ref=grouped.at[own * o + a, pl.ds(at, count)],
                send_sem=fwd_send.at[a, part],
                recv_sem=fwd_recv.at[a, part],
                device_id={"orb": to},
                device_id_type=MESH,
            ).start()

        pltpu.make_async_copy(
            third.at[o, a, pl.ds(at, count)],
            grouped.at[own * o + a, pl.ds(at, count)],
            fwd_own.at[a, part],
        ).start()

    def wait_cells(a, part):
        at, count = (0, half) if part == 0 else (half, 6)
        block = grouped.at[pl.ds(0, orbs - 1), pl.ds(at, count)]
        pltpu.make_async_copy(block, block, fwd_send.at[a, part]).wait()
        pltpu.make_async_copy(block, block, fwd_recv.at[a, part]).wait()
        single = grouped.at[0, pl.ds(at, count)]
        pltpu.make_async_copy(single, single, fwd_own.at[a, part]).wait()

    for a in range(own):
        for copy in halos[0][a]:
            copy.start()
    for copy in loads:
        copy.wait()

    @pl.loop(0, layers)
    def _(i):
        diag[i] = diag[i] * (1.0 / filter_half) + DIAGONAL

    for a in range(own):
        inner(0, a)
    for stage in range(3):
        for a in range(own):
            for copy in halos[stage][a]:
                copy.wait()
            outer(stage, a)
            if stage < 2:
                for copy in halos[stage + 1][a]:
                    copy.start()
                inner(stage + 1, a)
                if stage == 1:
                    to_cells(a, 0)
            else:
                to_cells(a, 1)

    flat = grouped.reshape(n * layers * chunk, nz)
    flat_back = back.reshape(n * layers * chunk, nz)
    stride = layers * chunk

    def split_slots(begin, end):
        def larger(slot, most):
            for r in range(chunk):
                most = jnp.maximum(most, jnp.abs(flat[pl.ds(slot * chunk + r, n, stride=stride), :]))
            return most

        most = lax.fori_loop(begin, end, larger, jnp.zeros((n, nz), F32), unroll=2)
        anchor = anchor_of(jnp.broadcast_to(jnp.max(most, axis=1, keepdims=True), (n, nz)))

        @pl.loop(begin, end, unroll=2)
        def _(slot):
            for r in range(chunk):
                row = slot * chunk + r
                x = flat[pl.ds(row, n, stride=stride), :]
                lanes = pl.ds(pl.multiple_of(row * nz, nz), nz)
                for part, value in enumerate(limbs(x, anchor)):
                    split_x[pl.ds(part * n, n), lanes] = value

    def gram_of(begin, end, pair):
        for slot in range(begin, end):
            x = split_x[:, slot * chunk * nz : (slot + 1) * chunk * nz]
            value = lax.dot_general(x, x, (((1,), (1,)), ((), ())), preferred_element_type=F32)
            if pair is None:
                pair = value, jnp.zeros_like(value)
            else:
                high, error = two_sum(pair[0], value)
                pair = high, pair[1] + error
        return pair

    lane = lax.broadcasted_iota(jnp.int32, (8, 128), 1)

    def total(pair):
        parts = [tuple(v[p * n : (p + 1) * n] for v in pair) for p in range(LIMBS)]
        low_first = add_pairs(add_pairs(parts[3], parts[2]), add_pairs(parts[1], parts[0]))
        pad = jnp.zeros((n, 128 - LIMBS * n), F32)
        wide = tuple(jnp.concatenate([v, pad], axis=1) for v in low_first)
        for step in (2 * n, n):
            wide = add_pairs(wide, tuple(pltpu.roll(v, 128 - step, 1) for v in wide))
        top, bottom = tuple(v[:8] for v in wide), tuple(pltpu.roll(v[8:], n, 1) for v in wide)
        high, low = (jnp.where(lane < n, t, b) for t, b in zip(top, bottom))
        packed = jnp.where(lane < 2 * n, high, pltpu.roll(low, 2 * n, 1))
        packed = jnp.where(lane < 4 * n, packed, 0.0)
        for which, (axis, count, me, buf) in enumerate((("orb", orbs, o, gram_orb), ("dom", doms, d, gram_dom))):
            buf[me] = packed

            @pl.loop(1, count)
            def _(p):
                pltpu.make_async_remote_copy(
                    src_ref=buf.at[me],
                    dst_ref=buf.at[me],
                    send_sem=gram_send.at[which],
                    recv_sem=gram_recv.at[which],
                    device_id={axis: lax.rem(me + p, count)},
                    device_id_type=MESH,
                ).start()

            block = buf.at[pl.ds(0, count - 1)]
            pltpu.make_async_copy(block, block, gram_recv.at[which]).wait()
            value, error = buf[...], None
            while count > 1:
                count //= 2
                value, extra = two_sum(value[:count], value[count:])
                error = extra if error is None else extra + (error[:count] + error[count:])
            packed = value[0] + jnp.where(lane >= 2 * n, pltpu.roll(error[0], 2 * n, 1), 0.0)
            packed = jnp.where(lane < 4 * n, packed, 0.0)
        low = pltpu.roll(packed, 128 - 2 * n, 1)
        pair = tuple(
            jnp.where(
                lax.broadcasted_iota(jnp.int32, (n, 128), 1) < n,
                jnp.concatenate([v, pltpu.roll(v, 128 - n, 1)], axis=0),
                0.0,
            )
            for v in (packed, low)
        )
        return two_sum(pair[0], pair[1])

    def stacked(matrix):
        wide = matrix
        for part in range(1, LIMBS):
            wide = wide + pltpu.roll(matrix, part * n, 1)
        return jnp.concatenate(split3(wide), axis=0)[:, : LIMBS * n]

    def applied(weights, lanes):
        full = jnp.dot(weights, split_x[:, lanes], preferred_element_type=F32)
        return full[0:n] + (full[n : 2 * n] + full[2 * n : 3 * n])

    for a in range(own):
        wait_cells(a, 0)
    split_slots(0, half)
    pair = gram_of(0, half, None)
    for a in range(own):
        wait_cells(a, 1)
    split_slots(half, layers)
    pair = gram_of(half, layers, pair)
    gram = total(pair)
    weights = stacked(combined(gram, float(cells), n))

    def send_back(part, at, count, layer):
        @pl.loop(1, orbs)
        def _(p):
            to = lax.rem(o + p, orbs)
            pltpu.make_async_remote_copy(
                src_ref=back.at[pl.ds(own * to, own), pl.ds(at, count)],
                dst_ref=out_ref.at[:, pl.ds(layer, count), pl.ds(chunk * o, chunk)],
                send_sem=bck_send.at[part],
                recv_sem=bck_recv.at[part],
                device_id={"orb": to},
                device_id_type=MESH,
            ).start()

        pltpu.make_async_copy(
            back.at[pl.ds(own * o, own), pl.ds(at, count)],
            out_ref.at[:, pl.ds(layer, count), pl.ds(chunk * o, chunk)],
            bck_own.at[part],
        ).start()

    parts = ((0, half, 3), (half, 3, half + 3), (half + 3, 3, 0))
    for part, (at, count, layer) in enumerate(parts):

        @pl.loop(at, at + count)
        def _(slot):
            lanes = pl.ds(pl.multiple_of(slot * chunk * nz, chunk * nz), chunk * nz)
            y = applied(weights, lanes)
            for r in range(chunk):
                flat_back[pl.ds(slot * chunk + r, n, stride=stride), :] = y[:, r * nz : (r + 1) * nz]

        send_back(part, at, count, layer)
    for part, (at, count, layer) in enumerate(parts):
        block = back.at[pl.ds(0, own * (orbs - 1)), pl.ds(at, count)]
        pltpu.make_async_copy(block, block, bck_send.at[part]).wait()
        pltpu.make_async_copy(block, block, bck_recv.at[part]).wait()
        single = back.at[pl.ds(0, own), pl.ds(at, count)]
        pltpu.make_async_copy(single, single, bck_own.at[part]).wait()
    for which, buf in enumerate((gram_orb, gram_dom)):
        block = buf.at[pl.ds(0, (orbs, doms)[which] - 1)]
        pltpu.make_async_copy(block, block, gram_send.at[which]).wait()


def on_device(orbitals, potential):
    own, layers, ny, nz = orbitals.shape
    doms, orbs = lax.axis_size("dom"), lax.axis_size("orb")
    n = own * orbs
    chunk = ny // orbs
    cells = layers * doms * ny * nz
    width = layers * chunk * nz
    dma = pltpu.SemaphoreType.DMA
    field = pltpu.VMEM((own, layers + 6, ny + 2 * PAD, nz), F32)
    return pl.pallas_call(
        functools.partial(kernel, (doms, orbs, own, layers, ny, nz, cells)),
        out_shape=jax.ShapeDtypeStruct(orbitals.shape, F32),
        in_specs=[pl.BlockSpec(memory_space=pl.ANY)] * 2,
        out_specs=pl.BlockSpec(memory_space=pl.ANY),
        scratch_shapes=[
            field,
            field,
            field,
            pltpu.VMEM((layers, ny, nz), F32),
            pltpu.VMEM((orbs, own, layers, chunk, nz), F32),
            pltpu.VMEM((n, layers, chunk, nz), F32),
            pltpu.VMEM((LIMBS * n, width), BF16),
            pltpu.VMEM((n, layers, chunk, nz), F32),
            pltpu.VMEM((orbs, 8, 128), F32),
            pltpu.VMEM((doms, 8, 128), F32),
            dma((1 + 3 * own,)),
            dma((3, own, 2)),
            dma((3, own, 2)),
            dma((own, 2)),
            dma((own, 2)),
            dma((own, 2)),
            dma((2,)),
            dma((2,)),
            dma((3,)),
            dma((3,)),
            dma((3,)),
        ],
        compiler_params=pltpu.CompilerParams(
            collective_id=0, has_side_effects=True, vmem_limit_bytes=60 * 1024 * 1024
        ),
        cost_estimate=pl.CostEstimate(flops=100_000_000, bytes_accessed=4_000_000, transcendentals=0),
    )(orbitals, potential)


def solution(mesh):
    return jax.shard_map(
        on_device,
        mesh=mesh,
        in_specs=(P("orb", "dom", None, None), P("dom", None, None)),
        out_specs=P("orb", "dom", None, None),
        check_vma=False,
    )
```

```python
import functools

import jax
import jax.numpy as jnp
from jax import lax
from jax.experimental import pallas as pl
from jax.experimental.pallas import tpu as pltpu
from jax.sharding import PartitionSpec as P

MESH = pl.DeviceIdType.MESH
F32 = jnp.float32
BF16 = jnp.bfloat16
coefficients = (-49.0 / 18.0, 1.5, -0.15, 1.0 / 90.0)
spacing = 0.5
filter_centre = 23.0
filter_half = 23.0
kinetic = -0.5 / (spacing * spacing) / filter_half
STEP = tuple(kinetic * c for c in coefficients)
DIAGONAL = 3.0 * STEP[0] - filter_centre / filter_half
LIMBS = 4


def split3(x):
    hi = x.astype(BF16)
    rest = x - hi.astype(F32)
    mid = rest.astype(BF16)
    low = (rest - mid.astype(F32)).astype(BF16)
    return hi, mid, low


def anchor_of(largest):
    shift = largest * 2.0**23
    return ((largest + shift) - shift) * (1.25 * 2.0**17)


def limbs(x, anchor):
    out = []
    for part in range(LIMBS):
        place = anchor * 2.0 ** (-8 * part)
        value = (x + place) - place
        x = x - value
        out.append(value.astype(BF16))
    return out


def two_sum(a, b):
    total = a + b
    part = total - a
    return total, (a - (total - part)) + (b - part)


def add_pairs(a, b):
    total, error = two_sum(a[0], b[0])
    return total, error + (a[1] + b[1])


def halves(x):
    wide = x * 4097.0
    high = wide - (wide - x)
    return high, x - high


def lane_of(x, j):
    return jnp.broadcast_to(x[:, j : j + 1], x.shape)


def row_of(x, j):
    return jnp.broadcast_to(x[j : j + 1, :], x.shape)


def product(left, right, n):
    left_high, left_low = halves(left[0])
    right_high, right_low = halves(right[0])
    total, low = None, None
    for k in range(n):
        a, ah, al = lane_of(left[0], k), lane_of(left_high, k), lane_of(left_low, k)
        b, bh, bl = row_of(right[0], k), row_of(right_high, k), row_of(right_low, k)
        value = a * b
        error = ((ah * bh - value) + ah * bl + al * bh) + al * bl
        if right[1] is not None:
            error = error + a * row_of(right[1], k)
        if left[1] is not None:
            error = error + lane_of(left[1], k) * b
        if total is None:
            total, low = value, error
        else:
            total, carry = two_sum(total, value)
            low = low + (carry + error)
    return total, low


def eliminate(gram, n):
    rows = lax.broadcasted_iota(jnp.int32, (n, 128), 0)
    lanes = lax.broadcasted_iota(jnp.int32, (n, 128), 1)
    work = jnp.where(lanes < n, gram, 0.0) + jnp.where(lanes == rows + n, 1.0, 0.0)
    for j in range(n - 1):
        column = lane_of(work, j)
        factor = jnp.where(rows > j, column / row_of(column, j), 0.0)
        work = work - factor * row_of(work, j)
    diagonal = jnp.sum(jnp.where(lanes == rows, work, 0.0), axis=1, keepdims=True)
    scaled = work / jnp.sqrt(jnp.broadcast_to(diagonal, (n, 128)))
    return jnp.where(lanes < n, pltpu.roll(scaled, 128 - n, 1), 0.0)


def combined(gram, cells, n):
    scale = 2.0**-20
    high, low = gram[0] * scale, gram[1] * scale
    rest = 1.0 / (cells * scale)
    inverse_one = eliminate(high * rest, n)
    turned = jnp.transpose(inverse_one)[:n]
    turned = jnp.concatenate([turned, jnp.zeros((n, 128 - n), F32)], axis=1)
    half = product((inverse_one, None), (high, low), n)
    gram_two = product(half, (turned, None), n)
    inverse_two = eliminate((gram_two[0] + gram_two[1]) * rest, n)
    both = lane_of(inverse_two, 0) * row_of(inverse_one, 0)
    for k in range(1, n):
        both = both + lane_of(inverse_two, k) * row_of(inverse_one, k)
    return both


def kernel(
    sizes,
    orb_ref,
    pot_ref,
    out_ref,
    e0,
    e1,
    e2,
    raw,
    diag,
    third,
    grouped,
    split_x,
    back,
    gram_orb,
    gram_dom,
    load_sem,
    halo_send,
    halo_recv,
    pot_send,
    pot_recv,
    fwd_send,
    fwd_recv,
    fwd_own,
    gram_send,
    gram_recv,
    bck_send,
    bck_recv,
    bck_own,
):
    doms, orbs, own, layers, ny, nz, cells = sizes
    n = own * orbs
    chunk = ny // orbs
    half = layers - 6
    d = lax.axis_index("dom")
    o = lax.axis_index("orb")
    left = lax.rem(d + doms - 1, doms)
    right = lax.rem(d + 1, doms)

    barrier = pltpu.get_barrier_semaphore()

    @pl.loop(1, orbs)
    def _(p):
        pl.semaphore_signal(
            barrier, inc=1, device_id={"orb": lax.rem(o + p, orbs)}, device_id_type=MESH
        )

    @pl.loop(1, doms)
    def _(p):
        pl.semaphore_signal(
            barrier, inc=1, device_id={"dom": lax.rem(d + p, doms)}, device_id_type=MESH
        )

    loads = [pltpu.make_async_copy(pot_ref, raw.at[pl.ds(6, layers)], load_sem.at[0])]
    for a in range(own):
        loads.append(pltpu.make_async_copy(orb_ref.at[a], e0.at[a, pl.ds(9, layers)], load_sem.at[1 + a]))
    for copy in loads:
        copy.start()

    pl.semaphore_wait(barrier, orbs - 1 + doms - 1)

    fields = (e0, e1, e2)

    def halo(piece, a):
        out = []
        for side, (at, to_at, to) in enumerate(
            ((layers - 3 - 3 * piece, 6 - 3 * piece, right), (3 * piece, layers + 9 + 3 * piece, left))
        ):
            out.append(
                pltpu.make_async_remote_copy(
                    src_ref=orb_ref.at[a, pl.ds(at, 3)],
                    dst_ref=e0.at[a, pl.ds(to_at, 3)],
                    send_sem=halo_send.at[a, piece, side],
                    recv_sem=halo_recv.at[a, piece, side],
                    device_id={"dom": to},
                    device_id_type=MESH,
                )
            )
        return out

    odd = lax.rem(o, 2)
    pair_device = o + 1 - 2 * odd

    def margin_copies():
        out = []
        for side, (at, to_at, to) in enumerate(
            ((layers - 3 - 3 * odd, 3 - 3 * odd, right), (3 * odd, layers + 6 + 3 * odd, left))
        ):
            taken = raw.at[pl.ds(to_at, 3)]
            across = pltpu.make_async_remote_copy(
                src_ref=pot_ref.at[pl.ds(at, 3)],
                dst_ref=taken,
                send_sem=pot_send.at[0, side],
                recv_sem=pot_recv.at[0, side],
                device_id={"dom": to},
                device_id_type=MESH,
            )
            within = pltpu.make_async_remote_copy(
                src_ref=taken,
                dst_ref=taken,
                send_sem=pot_send.at[1, side],
                recv_sem=pot_recv.at[1, side],
                device_id={"orb": pair_device},
                device_id_type=MESH,
            )
            out.append((across, within))
        return out

    margins = margin_copies()

    def start(copies):
        for copy in copies:
            copy.start()

    def wait(copies):
        for copy in copies:
            copy.wait()

    start(halo(0, 0))
    start([across for across, _ in margins])
    start(halo(1, 0))
    start(halo(2, 0))
    for a in range(1, own):
        for piece in range(3):
            start(halo(piece, a))

    def apply_layer(stage, a, layer):
        src = fields[stage]
        at = layer + 9 - 3 * stage
        centre = src[a, at]
        result = diag[layer + 6] * centre
        for k in range(1, 4):
            near = src[a, at + k] + src[a, at - k]
            near = near + (pltpu.roll(centre, k, 0) + pltpu.roll(centre, ny - k, 0))
            near = near + (pltpu.roll(centre, k, 1) + pltpu.roll(centre, nz - k, 1))
            result = result + STEP[k] * near
        if stage > 0:
            result = 2.0 * result - fields[stage - 1][a, at + 3]
        if stage < 2:
            fields[stage + 1][a, at - 3] = result
        else:
            third[:, a, (layer - 3) % layers] = result.reshape(orbs, chunk, nz)

    inner = range(3, layers - 3)

    def margin(step):
        return (*range(-3 * step, 3 - 3 * step), *range(layers - 3 + 3 * step, layers + 3 * step))

    def apply_layers(stage, a, chosen):
        for layer in chosen:
            apply_layer(stage, a, layer)

    def to_cells(a, part):
        at, count = (0, half) if part == 0 else (half, 6)

        @pl.loop(1, orbs)
        def _(p):
            to = lax.rem(o + p, orbs)
            pltpu.make_async_remote_copy(
                src_ref=third.at[to, a, pl.ds(at, count)],
                dst_ref=grouped.at[own * o + a, pl.ds(at, count)],
                send_sem=fwd_send.at[a, part],
                recv_sem=fwd_recv.at[a, part],
                device_id={"orb": to},
                device_id_type=MESH,
            ).start()

        pltpu.make_async_copy(
            third.at[o, a, pl.ds(at, count)],
            grouped.at[own * o + a, pl.ds(at, count)],
            fwd_own.at[a, part],
        ).start()

    def wait_cells(a, part):
        at, count = (0, half) if part == 0 else (half, 6)
        block = grouped.at[pl.ds(0, orbs - 1), pl.ds(at, count)]
        pltpu.make_async_copy(block, block, fwd_recv.at[a, part]).wait()
        single = grouped.at[0, pl.ds(at, count)]
        pltpu.make_async_copy(single, single, fwd_own.at[a, part]).wait()

    def weigh(begin, end):
        @pl.loop(begin, end)
        def _(i):
            diag[i] = raw[i] * (1.0 / filter_half) + DIAGONAL

    wait(loads)
    weigh(6, layers + 6)
    apply_layers(0, 0, inner)
    wait(halo(0, 0))
    apply_layers(0, 0, margin(0))
    apply_layers(1, 0, inner)
    for across, _ in margins:
        across.wait()
    for _, within in margins:
        within.start()
    for _, within in margins:
        within.wait()
    weigh(0, 6)
    weigh(layers + 6, layers + 12)

    def rest(a):
        wait(halo(1, a))
        apply_layers(0, a, margin(1))
        apply_layers(1, a, margin(0))
        apply_layers(2, a, inner)
        to_cells(a, 0)
        wait(halo(2, a))
        apply_layers(0, a, margin(2))
        apply_layers(1, a, margin(1))
        apply_layers(2, a, margin(0))
        to_cells(a, 1)

    rest(0)
    for a in range(1, own):
        apply_layers(0, a, inner)
        wait(halo(0, a))
        apply_layers(0, a, margin(0))
        apply_layers(1, a, inner)
        rest(a)

    flat = grouped.reshape(n * layers * chunk, nz)
    flat_back = back.reshape(n * layers * chunk, nz)
    stride = layers * chunk

    def split_slots(begin, end):
        def larger(slot, most):
            for r in range(chunk):
                most = jnp.maximum(most, jnp.abs(flat[pl.ds(slot * chunk + r, n, stride=stride), :]))
            return most

        most = lax.fori_loop(begin, end, larger, jnp.zeros((n, nz), F32), unroll=2)
        anchor = anchor_of(jnp.broadcast_to(jnp.max(most, axis=1, keepdims=True), (n, nz)))

        @pl.loop(begin, end, unroll=2)
        def _(slot):
            for r in range(chunk):
                row = slot * chunk + r
                x = flat[pl.ds(row, n, stride=stride), :]
                lanes = pl.ds(pl.multiple_of(row * nz, nz), nz)
                for part, value in enumerate(limbs(x, anchor)):
                    split_x[pl.ds(part * n, n), lanes] = value

    def gram_of(begin, end, pair):
        for slot in range(begin, end):
            x = split_x[:, slot * chunk * nz : (slot + 1) * chunk * nz]
            value = lax.dot_general(x, x, (((1,), (1,)), ((), ())), preferred_element_type=F32)
            if pair is None:
                pair = value, jnp.zeros_like(value)
            else:
                high, error = two_sum(pair[0], value)
                pair = high, pair[1] + error
        return pair

    lane = lax.broadcasted_iota(jnp.int32, (8, 128), 1)
    lane4 = lax.broadcasted_iota(jnp.int32, (4, 128), 1)
    lows = (lane4 & 32) == 32

    def total(pair):
        parts = [tuple(v[p * n : (p + 1) * n] for v in pair) for p in range(LIMBS)]
        low_first = add_pairs(add_pairs(parts[3], parts[2]), add_pairs(parts[1], parts[0]))
        pad = jnp.zeros((n, 128 - LIMBS * n), F32)
        wide = tuple(jnp.concatenate([v, pad], axis=1) for v in low_first)
        for step in (2 * n, n):
            wide = add_pairs(wide, tuple(pltpu.roll(v, 128 - step, 1) for v in wide))
        top, bottom = tuple(v[:8] for v in wide), tuple(pltpu.roll(v[8:], n, 1) for v in wide)
        high, low = (jnp.where(lane < n, t, b) for t, b in zip(top, bottom))
        packed = jnp.where(lane < 2 * n, high, pltpu.roll(low, 2 * n, 1))
        packed = jnp.where(lane4 < 64, packed[:4], pltpu.roll(packed, 64, 1)[4:])
        for which, (axis, count, me, buf) in enumerate((("orb", orbs, o, gram_orb), ("dom", doms, d, gram_dom))):
            buf[me] = packed

            @pl.loop(1, count)
            def _(p):
                pltpu.make_async_remote_copy(
                    src_ref=buf.at[me],
                    dst_ref=buf.at[me],
                    send_sem=gram_send.at[which],
                    recv_sem=gram_recv.at[which],
                    device_id={axis: lax.rem(me + p, count)},
                    device_id_type=MESH,
                ).start()

            block = buf.at[pl.ds(0, count - 1)]
            pltpu.make_async_copy(block, block, gram_recv.at[which]).wait()
            value, error = buf[...], None
            while count > 1:
                count //= 2
                value, extra = two_sum(value[:count], value[count:])
                error = extra if error is None else extra + (error[:count] + error[count:])
            packed = value[0] + jnp.where(lows, pltpu.roll(error[0], 2 * n, 1), 0.0)
        packed = jnp.concatenate([packed, pltpu.roll(packed, 64, 1)], axis=0)
        low = pltpu.roll(packed, 128 - 2 * n, 1)
        pair = tuple(
            jnp.where(
                lax.broadcasted_iota(jnp.int32, (n, 128), 1) < n,
                jnp.concatenate([v, pltpu.roll(v, 128 - n, 1)], axis=0),
                0.0,
            )
            for v in (packed, low)
        )
        return two_sum(pair[0], pair[1])

    def stacked(matrix):
        wide = matrix
        for part in range(1, LIMBS):
            wide = wide + pltpu.roll(matrix, part * n, 1)
        return jnp.concatenate(split3(wide), axis=0)[:, : LIMBS * n]

    def applied(weights, lanes):
        full = jnp.dot(weights, split_x[:, lanes], preferred_element_type=F32)
        return full[0:n] + (full[n : 2 * n] + full[2 * n : 3 * n])

    for a in range(own):
        wait_cells(a, 0)
    split_slots(0, half)
    pair = gram_of(0, half, None)
    for a in range(own):
        wait_cells(a, 1)
    split_slots(half, layers)
    pair = gram_of(half, layers, pair)
    gram = total(pair)
    weights = stacked(combined(gram, float(cells), n))

    def send_back(part, at, count, layer):
        @pl.loop(1, orbs)
        def _(p):
            to = lax.rem(o + p, orbs)
            pltpu.make_async_remote_copy(
                src_ref=back.at[pl.ds(own * to, own), pl.ds(at, count)],
                dst_ref=out_ref.at[:, pl.ds(layer, count), pl.ds(chunk * o, chunk)],
                send_sem=bck_send.at[part],
                recv_sem=bck_recv.at[part],
                device_id={"orb": to},
                device_id_type=MESH,
            ).start()

        pltpu.make_async_copy(
            back.at[pl.ds(own * o, own), pl.ds(at, count)],
            out_ref.at[:, pl.ds(layer, count), pl.ds(chunk * o, chunk)],
            bck_own.at[part],
        ).start()

    parts = ((0, half, 3), (half, 3, half + 3), (half + 3, 3, 0))
    for part, (at, count, layer) in enumerate(parts):

        @pl.loop(at, at + count)
        def _(slot):
            lanes = pl.ds(pl.multiple_of(slot * chunk * nz, chunk * nz), chunk * nz)
            y = applied(weights, lanes)
            for r in range(chunk):
                flat_back[pl.ds(slot * chunk + r, n, stride=stride), :] = y[:, r * nz : (r + 1) * nz]

        send_back(part, at, count, layer)
    for part, (at, count, layer) in enumerate(parts):
        block = back.at[pl.ds(0, own * (orbs - 1)), pl.ds(at, count)]
        pltpu.make_async_copy(block, block, bck_send.at[part]).wait()
        pltpu.make_async_copy(block, block, bck_recv.at[part]).wait()
        single = back.at[pl.ds(0, own), pl.ds(at, count)]
        pltpu.make_async_copy(single, single, bck_own.at[part]).wait()
    for a in range(own):
        for part, (at, count) in enumerate(((0, half), (half, 6))):
            block = grouped.at[pl.ds(0, orbs - 1), pl.ds(at, count)]
            pltpu.make_async_copy(block, block, fwd_send.at[a, part]).wait()
    for which, buf in enumerate((gram_orb, gram_dom)):
        block = buf.at[pl.ds(0, (orbs, doms)[which] - 1)]
        pltpu.make_async_copy(block, block, gram_send.at[which]).wait()


def on_device(orbitals, potential):
    own, layers, ny, nz = orbitals.shape
    doms, orbs = lax.axis_size("dom"), lax.axis_size("orb")
    n = own * orbs
    chunk = ny // orbs
    cells = layers * doms * ny * nz
    width = layers * chunk * nz
    dma = pltpu.SemaphoreType.DMA

    def field(extra):
        return pltpu.VMEM((own, layers + extra, ny, nz), F32)

    return pl.pallas_call(
        functools.partial(kernel, (doms, orbs, own, layers, ny, nz, cells)),
        out_shape=pltpu.VMEM(orbitals.shape, F32),
        in_specs=[pl.BlockSpec(memory_space=pltpu.HBM)] * 2,
        out_specs=pl.BlockSpec(memory_space=pltpu.VMEM),
        scratch_shapes=[
            field(18),
            field(12),
            field(6),
            pltpu.VMEM((layers + 12, ny, nz), F32),
            pltpu.VMEM((layers + 12, ny, nz), F32),
            pltpu.VMEM((orbs, own, layers, chunk, nz), F32),
            pltpu.VMEM((n, layers, chunk, nz), F32),
            pltpu.VMEM((LIMBS * n, width), BF16),
            pltpu.VMEM((n, layers, chunk, nz), F32),
            pltpu.VMEM((orbs, 4, 128), F32),
            pltpu.VMEM((doms, 4, 128), F32),
            dma((1 + own,)),
            dma((own, 3, 2)),
            dma((own, 3, 2)),
            dma((2, 2)),
            dma((2, 2)),
            dma((own, 2)),
            dma((own, 2)),
            dma((own, 2)),
            dma((2,)),
            dma((2,)),
            dma((3,)),
            dma((3,)),
            dma((3,)),
        ],
        compiler_params=pltpu.CompilerParams(
            collective_id=0, has_side_effects=True, vmem_limit_bytes=40 * 1024 * 1024
        ),
        cost_estimate=pl.CostEstimate(flops=100_000_000, bytes_accessed=4_000_000, transcendentals=0),
    )(*(pltpu.with_memory_space_constraint(v, pltpu.HBM) for v in (orbitals, potential)))


def solution(mesh):
    return jax.shard_map(
        on_device,
        mesh=mesh,
        in_specs=(P("orb", "dom", None, None), P("dom", None, None)),
        out_specs=P("orb", "dom", None, None),
        check_vma=False,
    )
```

```python
import functools

import jax
import jax.numpy as jnp
from jax import lax
from jax.experimental import pallas as pl
from jax.experimental.pallas import tpu as pltpu
from jax.sharding import PartitionSpec as P

MESH = pl.DeviceIdType.MESH
F32 = jnp.float32
BF16 = jnp.bfloat16
coefficients = (-49.0 / 18.0, 1.5, -0.15, 1.0 / 90.0)
spacing = 0.5
filter_centre = 23.0
filter_half = 23.0
kinetic = -0.5 / (spacing * spacing) / filter_half
STEP = tuple(kinetic * c for c in coefficients)
DIAGONAL = 3.0 * STEP[0] - filter_centre / filter_half
LIMBS = 4


def split3(x):
    hi = x.astype(BF16)
    rest = x - hi.astype(F32)
    mid = rest.astype(BF16)
    low = (rest - mid.astype(F32)).astype(BF16)
    return hi, mid, low


def anchor_of(largest):
    shift = largest * 2.0**23
    return ((largest + shift) - shift) * (1.25 * 2.0**17)


def limbs(x, anchor):
    out = []
    for part in range(LIMBS):
        place = anchor * 2.0 ** (-8 * part)
        value = (x + place) - place
        x = x - value
        out.append(value.astype(BF16))
    return out


def two_sum(a, b):
    total = a + b
    part = total - a
    return total, (a - (total - part)) + (b - part)


def add_pairs(a, b):
    total, error = two_sum(a[0], b[0])
    return total, error + (a[1] + b[1])


def halves(x):
    wide = x * 4097.0
    high = wide - (wide - x)
    return high, x - high


def lane_of(x, j):
    return jnp.broadcast_to(x[:, j : j + 1], x.shape)


def row_of(x, j):
    return jnp.broadcast_to(x[j : j + 1, :], x.shape)


def product(left, right, n):
    left_high, left_low = halves(left[0])
    right_high, right_low = halves(right[0])
    total, low = None, None
    for k in range(n):
        a, ah, al = lane_of(left[0], k), lane_of(left_high, k), lane_of(left_low, k)
        b, bh, bl = row_of(right[0], k), row_of(right_high, k), row_of(right_low, k)
        value = a * b
        error = ((ah * bh - value) + ah * bl + al * bh) + al * bl
        if right[1] is not None:
            error = error + a * row_of(right[1], k)
        if left[1] is not None:
            error = error + lane_of(left[1], k) * b
        if total is None:
            total, low = value, error
        else:
            total, carry = two_sum(total, value)
            low = low + (carry + error)
    return total, low


def eliminate(gram, n):
    rows = lax.broadcasted_iota(jnp.int32, (n, 128), 0)
    lanes = lax.broadcasted_iota(jnp.int32, (n, 128), 1)
    work = jnp.where(lanes < n, gram, 0.0) + jnp.where(lanes == rows + n, 1.0, 0.0)
    for j in range(0, n, 2):
        first, second = lane_of(work, j), lane_of(work, j + 1)
        row, next_row = row_of(work, j), row_of(work, j + 1)
        a, b, c, d = row_of(first, j), row_of(second, j), row_of(first, j + 1), row_of(second, j + 1)
        over = 1.0 / a
        over_next = a / (a * d - b * c)
        factor = first * over
        next_factor = jnp.where(rows > j + 1, (second - factor * b) * over_next, 0.0)
        next_row = next_row - (c * over) * row
        work = work - jnp.where(rows > j, factor, 0.0) * row - next_factor * next_row
    diagonal = jnp.sum(jnp.where(lanes == rows, work, 0.0), axis=1, keepdims=True)
    scaled = work / jnp.sqrt(jnp.broadcast_to(diagonal, (n, 128)))
    return jnp.where(lanes < n, pltpu.roll(scaled, 128 - n, 1), 0.0)


def combined(gram, cells, n):
    scale = 2.0**-20
    high, low = gram[0] * scale, gram[1] * scale
    rest = 1.0 / (cells * scale)
    inverse_one = eliminate(high * rest, n)
    turned = jnp.transpose(inverse_one)[:n]
    turned = jnp.concatenate([turned, jnp.zeros((n, 128 - n), F32)], axis=1)
    half = product((inverse_one, None), (high, low), n)
    gram_two = product(half, (turned, None), n)
    inverse_two = eliminate((gram_two[0] + gram_two[1]) * rest, n)
    both = lane_of(inverse_two, 0) * row_of(inverse_one, 0)
    for k in range(1, n):
        both = both + lane_of(inverse_two, k) * row_of(inverse_one, k)
    return both


def kernel(
    sizes,
    orb_ref,
    pot_ref,
    out_ref,
    e0,
    e1,
    e2,
    raw,
    diag,
    third,
    grouped,
    split_x,
    back,
    gram_orb,
    gram_dom,
    load_sem,
    halo_send,
    halo_recv,
    pot_send,
    pot_recv,
    fwd_send,
    fwd_recv,
    gram_send,
    gram_recv,
    bck_send,
    bck_recv,
    bck_own,
):
    doms, orbs, own, layers, ny, nz, cells = sizes
    n = own * orbs
    chunk = ny // orbs
    half = layers - 6
    d = lax.axis_index("dom")
    o = lax.axis_index("orb")
    left = lax.rem(d + doms - 1, doms)
    right = lax.rem(d + 1, doms)

    barrier = pltpu.get_barrier_semaphore()

    @pl.loop(1, orbs)
    def _(p):
        pl.semaphore_signal(
            barrier, inc=1, device_id={"orb": lax.rem(o + p, orbs)}, device_id_type=MESH
        )

    @pl.loop(1, doms)
    def _(p):
        pl.semaphore_signal(
            barrier, inc=1, device_id={"dom": lax.rem(d + p, doms)}, device_id_type=MESH
        )

    loads = [pltpu.make_async_copy(pot_ref, raw.at[pl.ds(6, layers)], load_sem.at[0])]
    for a in range(own):
        loads.append(pltpu.make_async_copy(orb_ref.at[a], e0.at[a, pl.ds(9, layers)], load_sem.at[1 + a]))
    for copy in loads:
        copy.start()

    pl.semaphore_wait(barrier, orbs - 1 + doms - 1)

    fields = (e0, e1, e2)

    def halo(a, begin, end):
        out = []
        for side, (at, to_at, to) in enumerate(
            ((layers - end, 9 - end, right), (begin, layers + 9 + begin, left))
        ):
            out.append(
                pltpu.make_async_remote_copy(
                    src_ref=orb_ref.at[a, pl.ds(at, end - begin)],
                    dst_ref=e0.at[a, pl.ds(to_at, end - begin)],
                    send_sem=halo_send.at[a, begin // 3 + begin // 8, side],
                    recv_sem=halo_recv.at[a, begin // 3 + begin // 8, side],
                    device_id={"dom": to},
                    device_id_type=MESH,
                )
            )
        return out

    mine = pl.ds(chunk * o, chunk)
    across = []
    for side, (at, to_at, to) in enumerate(((layers - 6, 0, right), (0, layers + 6, left))):
        across.append(
            pltpu.make_async_remote_copy(
                src_ref=pot_ref.at[pl.ds(at, 6), mine],
                dst_ref=raw.at[pl.ds(to_at, 6), mine],
                send_sem=pot_send.at[0, side],
                recv_sem=pot_recv.at[0, side],
                device_id={"dom": to},
                device_id_type=MESH,
            )
        )

    def share_margins():
        for side, at in enumerate((0, layers + 6)):

            @pl.loop(1, orbs)
            def _(p):
                pltpu.make_async_remote_copy(
                    src_ref=raw.at[pl.ds(at, 6), mine],
                    dst_ref=raw.at[pl.ds(at, 6), mine],
                    send_sem=pot_send.at[1, side],
                    recv_sem=pot_recv.at[1, side],
                    device_id={"orb": lax.rem(o + p, orbs)},
                    device_id_type=MESH,
                ).start()

    def wait_margins(sems):
        for side in range(2):
            block = raw.at[pl.ds(0, 6), pl.ds(0, ny - chunk)]
            pltpu.make_async_copy(block, block, sems.at[1, side]).wait()

    def start(copies):
        for copy in copies:
            copy.start()

    def wait(copies):
        for copy in copies:
            copy.wait()

    reach = [(0, 3), (3, 6), (6, 9)]
    pieces = [reach] * (own - 1) + [reach[:2] + [(6, 8), (8, 9)]]
    start(across)
    for a in range(own):
        for begin, end in pieces[a]:
            start(halo(a, begin, end))

    def apply_layer(stage, a, layer):
        src = fields[stage]
        at = layer + 9 - 3 * stage
        centre = src[a, at]
        result = diag[layer + 6] * centre
        for k in range(1, 4):
            near = src[a, at + k] + src[a, at - k]
            near = near + (pltpu.roll(centre, k, 0) + pltpu.roll(centre, ny - k, 0))
            near = near + (pltpu.roll(centre, k, 1) + pltpu.roll(centre, nz - k, 1))
            result = result + STEP[k] * near
        if stage > 0:
            result = 2.0 * result - fields[stage - 1][a, at + 3]
        if stage < 2:
            fields[stage + 1][a, at - 3] = result
        else:
            third[:, a, (layer - 3) % layers] = result.reshape(orbs, chunk, nz)

    inner = range(3, layers - 3)

    def newly(stage, a, begin, end):
        low, high = 3 * (stage + 1), layers - 3 * (stage + 1)
        for layer in (*range(low - end, low - begin), *range(high + begin, high + end)):
            apply_layer(stage, a, layer)

    slots_of = {(3, 6): ((0, half),), (6, 9): ((half, 6),), (6, 8): ((half, 2), (half + 4, 2)), (8, 9): ((half + 2, 2),)}

    def to_cells(a, piece):
        part = pieces[a].index(piece) - 1
        for at, count in slots_of[piece]:

            @pl.loop(1, orbs)
            def _(p):
                to = lax.rem(o + p, orbs)
                pltpu.make_async_remote_copy(
                    src_ref=third.at[to, a, pl.ds(at, count)],
                    dst_ref=grouped.at[own * o + a, pl.ds(at, count)],
                    send_sem=fwd_send.at[a, part],
                    recv_sem=fwd_recv.at[a, part],
                    device_id={"orb": to},
                    device_id_type=MESH,
                ).start()

        for at, count in slots_of[piece]:
            for slot in range(at, at + count):
                grouped[own * o + a, slot] = third[o, a, slot]

    def wait_cells(a, part, sems):
        count = sum(count for _, count in slots_of[pieces[a][part + 1]])
        block = grouped.at[pl.ds(0, orbs - 1), pl.ds(0, count)]
        pltpu.make_async_copy(block, block, sems.at[a, part]).wait()

    def weigh(begin, end):
        @pl.loop(begin, end)
        def _(i):
            diag[i] = raw[i] * (1.0 / filter_half) + DIAGONAL

    wait(loads)
    weigh(6, layers + 6)
    for layer in inner:
        apply_layer(0, 0, layer)
    for copy in across:
        copy.wait()
    share_margins()
    for a in range(own):
        if a > 0:
            for layer in inner:
                apply_layer(0, a, layer)
        for begin, end in pieces[a]:
            wait(halo(a, begin, end))
            if a == 0 and begin == 3:
                wait_margins(pot_recv)
                weigh(0, 6)
                weigh(layers + 6, layers + 12)
            newly(0, a, begin, end)
            newly(1, a, begin, end)
            if begin > 0:
                newly(2, a, begin, end)
                to_cells(a, (begin, end))

    flat = grouped.reshape(n * layers * chunk, nz)
    flat_back = back.reshape(n * layers * chunk, nz)
    stride = layers * chunk

    def split_slots(ranges):
        def larger(slot, most):
            for r in range(chunk):
                most = jnp.maximum(most, jnp.abs(flat[pl.ds(slot * chunk + r, n, stride=stride), :]))
            return most

        most = jnp.zeros((n, nz), F32)
        for at, count in ranges:
            most = lax.fori_loop(at, at + count, larger, most, unroll=2)
        anchor = anchor_of(jnp.broadcast_to(jnp.max(most, axis=1, keepdims=True), (n, nz)))

        for at, count in ranges:

            @pl.loop(at, at + count, unroll=2)
            def _(slot):
                for r in range(chunk):
                    row = slot * chunk + r
                    x = flat[pl.ds(row, n, stride=stride), :]
                    lanes = pl.ds(pl.multiple_of(row * nz, nz), nz)
                    for part, value in enumerate(limbs(x, anchor)):
                        split_x[pl.ds(part * n, n), lanes] = value

    def gram_of(ranges, pair):
        for slot in (slot for at, count in ranges for slot in range(at, at + count)):
            x = split_x[:, slot * chunk * nz : (slot + 1) * chunk * nz]
            value = lax.dot_general(x, x, (((1,), (1,)), ((), ())), preferred_element_type=F32)
            if pair is None:
                pair = value, jnp.zeros_like(value)
            else:
                high, error = two_sum(pair[0], value)
                pair = high, pair[1] + error
        return pair

    lane = lax.broadcasted_iota(jnp.int32, (8, 128), 1)
    lane4 = lax.broadcasted_iota(jnp.int32, (4, 128), 1)
    lows = (lane4 & 32) == 32

    def total(pair):
        parts = [tuple(v[p * n : (p + 1) * n] for v in pair) for p in range(LIMBS)]
        low_first = add_pairs(add_pairs(parts[3], parts[2]), add_pairs(parts[1], parts[0]))
        pad = jnp.zeros((n, 128 - LIMBS * n), F32)
        wide = tuple(jnp.concatenate([v, pad], axis=1) for v in low_first)
        for step in (2 * n, n):
            wide = add_pairs(wide, tuple(pltpu.roll(v, 128 - step, 1) for v in wide))
        top, bottom = tuple(v[:8] for v in wide), tuple(pltpu.roll(v[8:], n, 1) for v in wide)
        high, low = (jnp.where(lane < n, t, b) for t, b in zip(top, bottom))
        packed = jnp.where(lane < 2 * n, high, pltpu.roll(low, 2 * n, 1))
        packed = jnp.where(lane4 < 64, packed[:4], pltpu.roll(packed, 64, 1)[4:])
        for which, (axis, count, me, buf) in enumerate((("orb", orbs, o, gram_orb), ("dom", doms, d, gram_dom))):
            buf[me] = packed

            @pl.loop(1, count)
            def _(p):
                pltpu.make_async_remote_copy(
                    src_ref=buf.at[me],
                    dst_ref=buf.at[me],
                    send_sem=gram_send.at[which],
                    recv_sem=gram_recv.at[which],
                    device_id={axis: lax.rem(me + p, count)},
                    device_id_type=MESH,
                ).start()

            block = buf.at[pl.ds(0, count - 1)]
            pltpu.make_async_copy(block, block, gram_recv.at[which]).wait()
            value, error = buf[...], None
            while count > 1:
                count //= 2
                value, extra = two_sum(value[:count], value[count:])
                error = extra if error is None else extra + (error[:count] + error[count:])
            packed = value[0] + jnp.where(lows, pltpu.roll(error[0], 2 * n, 1), 0.0)
        packed = jnp.concatenate([packed, pltpu.roll(packed, 64, 1)], axis=0)
        low = pltpu.roll(packed, 128 - 2 * n, 1)
        pair = tuple(
            jnp.where(
                lax.broadcasted_iota(jnp.int32, (n, 128), 1) < n,
                jnp.concatenate([v, pltpu.roll(v, 128 - n, 1)], axis=0),
                0.0,
            )
            for v in (packed, low)
        )
        return two_sum(pair[0], pair[1])

    def stacked(matrix):
        wide = matrix
        for part in range(1, LIMBS):
            wide = wide + pltpu.roll(matrix, part * n, 1)
        return jnp.concatenate(split3(wide), axis=0)[:, : LIMBS * n]

    def applied(weights, lanes):
        full = jnp.dot(weights, split_x[:, lanes], preferred_element_type=F32)
        return full[0:n] + (full[n : 2 * n] + full[2 * n : 3 * n])

    pair = None
    for part in range(3):
        for a in range(own):
            if part < len(pieces[a]) - 1:
                wait_cells(a, part, fwd_recv)
        ranges = slots_of[pieces[-1][part + 1]]
        split_slots(ranges)
        pair = gram_of(ranges, pair)
    gram = total(pair)
    weights = stacked(combined(gram, float(cells), n))

    def send_back(part, at, count, layer):
        @pl.loop(1, orbs)
        def _(p):
            to = lax.rem(o + p, orbs)
            pltpu.make_async_remote_copy(
                src_ref=back.at[pl.ds(own * to, own), pl.ds(at, count)],
                dst_ref=out_ref.at[:, pl.ds(layer, count), pl.ds(chunk * o, chunk)],
                send_sem=bck_send.at[part],
                recv_sem=bck_recv.at[part],
                device_id={"orb": to},
                device_id_type=MESH,
            ).start()

        pltpu.make_async_copy(
            back.at[pl.ds(own * o, own), pl.ds(at, count)],
            out_ref.at[:, pl.ds(layer, count), pl.ds(chunk * o, chunk)],
            bck_own.at[part],
        ).start()

    parts = ((0, half, 3), (half, 3, half + 3), (half + 3, 3, 0))
    for part, (at, count, layer) in enumerate(parts):

        @pl.loop(at, at + count)
        def _(slot):
            lanes = pl.ds(pl.multiple_of(slot * chunk * nz, chunk * nz), chunk * nz)
            y = applied(weights, lanes)
            for r in range(chunk):
                flat_back[pl.ds(slot * chunk + r, n, stride=stride), :] = y[:, r * nz : (r + 1) * nz]

        send_back(part, at, count, layer)
    for part, (at, count, layer) in enumerate(parts):
        block = back.at[pl.ds(0, own * (orbs - 1)), pl.ds(at, count)]
        pltpu.make_async_copy(block, block, bck_send.at[part]).wait()
        pltpu.make_async_copy(block, block, bck_recv.at[part]).wait()
        single = back.at[pl.ds(0, own), pl.ds(at, count)]
        pltpu.make_async_copy(single, single, bck_own.at[part]).wait()
    wait_margins(pot_send)
    for a in range(own):
        for part in range(len(pieces[a]) - 1):
            wait_cells(a, part, fwd_send)
    for which, buf in enumerate((gram_orb, gram_dom)):
        block = buf.at[pl.ds(0, (orbs, doms)[which] - 1)]
        pltpu.make_async_copy(block, block, gram_send.at[which]).wait()


def on_device(orbitals, potential):
    own, layers, ny, nz = orbitals.shape
    doms, orbs = lax.axis_size("dom"), lax.axis_size("orb")
    n = own * orbs
    chunk = ny // orbs
    cells = layers * doms * ny * nz
    width = layers * chunk * nz
    dma = pltpu.SemaphoreType.DMA

    def field(extra):
        return pltpu.VMEM((own, layers + extra, ny, nz), F32)

    return pl.pallas_call(
        functools.partial(kernel, (doms, orbs, own, layers, ny, nz, cells)),
        out_shape=pltpu.VMEM(orbitals.shape, F32),
        in_specs=[pl.BlockSpec(memory_space=pltpu.HBM)] * 2,
        out_specs=pl.BlockSpec(memory_space=pltpu.VMEM),
        scratch_shapes=[
            field(18),
            field(12),
            field(6),
            pltpu.VMEM((layers + 12, ny, nz), F32),
            pltpu.VMEM((layers + 12, ny, nz), F32),
            pltpu.VMEM((orbs, own, layers, chunk, nz), F32),
            pltpu.VMEM((n, layers, chunk, nz), F32),
            pltpu.VMEM((LIMBS * n, width), BF16),
            pltpu.VMEM((n, layers, chunk, nz), F32),
            pltpu.VMEM((orbs, 4, 128), F32),
            pltpu.VMEM((doms, 4, 128), F32),
            dma((1 + own,)),
            dma((own, 4, 2)),
            dma((own, 4, 2)),
            dma((2, 2)),
            dma((2, 2)),
            dma((own, 3)),
            dma((own, 3)),
            dma((2,)),
            dma((2,)),
            dma((3,)),
            dma((3,)),
            dma((3,)),
        ],
        compiler_params=pltpu.CompilerParams(
            collective_id=0, has_side_effects=True, vmem_limit_bytes=40 * 1024 * 1024
        ),
        cost_estimate=pl.CostEstimate(flops=100_000_000, bytes_accessed=4_000_000, transcendentals=0),
    )(*(pltpu.with_memory_space_constraint(v, pltpu.HBM) for v in (orbitals, potential)))


def solution(mesh):
    return jax.shard_map(
        on_device,
        mesh=mesh,
        in_specs=(P("orb", "dom", None, None), P("dom", None, None)),
        out_specs=P("orb", "dom", None, None),
        check_vma=False,
    )
```

```python
import functools

import jax
import jax.numpy as jnp
from jax import lax
from jax.experimental import pallas as pl
from jax.experimental.pallas import tpu as pltpu
from jax.sharding import PartitionSpec as P

MESH = pl.DeviceIdType.MESH
F32 = jnp.float32
BF16 = jnp.bfloat16
coefficients = (-49.0 / 18.0, 1.5, -0.15, 1.0 / 90.0)
spacing = 0.5
filter_centre = 23.0
filter_half = 23.0
kinetic = -0.5 / (spacing * spacing) / filter_half
STEP = tuple(kinetic * c for c in coefficients)
DIAGONAL = 3.0 * STEP[0] - filter_centre / filter_half
LIMBS = 4
EARLY = 2


def split3(x):
    hi = x.astype(BF16)
    rest = x - hi.astype(F32)
    mid = rest.astype(BF16)
    low = (rest - mid.astype(F32)).astype(BF16)
    return hi, mid, low


def anchor_of(largest):
    shift = largest * 2.0**23
    return ((largest + shift) - shift) * (1.25 * 2.0**17)


def limbs(x, anchor):
    out = []
    for part in range(LIMBS):
        place = anchor * 2.0 ** (-8 * part)
        value = (x + place) - place
        x = x - value
        out.append(value.astype(BF16))
    return out


def two_sum(a, b):
    total = a + b
    part = total - a
    return total, (a - (total - part)) + (b - part)


def add_pairs(a, b):
    total, error = two_sum(a[0], b[0])
    return total, error + (a[1] + b[1])


def halves(x):
    wide = x * 4097.0
    high = wide - (wide - x)
    return high, x - high


def lane_of(x, j):
    return jnp.broadcast_to(x[:, j : j + 1], x.shape)


def row_of(x, j):
    return jnp.broadcast_to(x[j : j + 1, :], x.shape)


def product(left, right, n):
    left_high, left_low = halves(left[0])
    right_high, right_low = halves(right[0])
    total, low = None, None
    for k in range(n):
        a, ah, al = lane_of(left[0], k), lane_of(left_high, k), lane_of(left_low, k)
        b, bh, bl = row_of(right[0], k), row_of(right_high, k), row_of(right_low, k)
        value = a * b
        error = ((ah * bh - value) + ah * bl + al * bh) + al * bl
        if right[1] is not None:
            error = error + a * row_of(right[1], k)
        if left[1] is not None:
            error = error + lane_of(left[1], k) * b
        if total is None:
            total, low = value, error
        else:
            total, carry = two_sum(total, value)
            low = low + (carry + error)
    return total, low


def eliminate(gram, n):
    rows = lax.broadcasted_iota(jnp.int32, (n, 128), 0)
    lanes = lax.broadcasted_iota(jnp.int32, (n, 128), 1)
    work = jnp.where(lanes < n, gram, 0.0) + jnp.where(lanes == rows + n, 1.0, 0.0)
    for j in range(0, n, 2):
        first, second = lane_of(work, j), lane_of(work, j + 1)
        row, next_row = row_of(work, j), row_of(work, j + 1)
        a, b, c, d = row_of(first, j), row_of(second, j), row_of(first, j + 1), row_of(second, j + 1)
        over = 1.0 / a
        over_next = a / (a * d - b * c)
        factor = first * over
        next_factor = jnp.where(rows > j + 1, (second - factor * b) * over_next, 0.0)
        next_row = next_row - (c * over) * row
        work = work - jnp.where(rows > j, factor, 0.0) * row - next_factor * next_row
    diagonal = jnp.sum(jnp.where(lanes == rows, work, 0.0), axis=1, keepdims=True)
    scaled = work / jnp.sqrt(jnp.broadcast_to(diagonal, (n, 128)))
    return jnp.where(lanes < n, pltpu.roll(scaled, 128 - n, 1), 0.0)


def combined(gram, cells, n):
    scale = 2.0**-20
    high, low = gram[0] * scale, gram[1] * scale
    rest = 1.0 / (cells * scale)
    inverse_one = eliminate(high * rest, n)
    turned = jnp.transpose(inverse_one)[:n]
    turned = jnp.concatenate([turned, jnp.zeros((n, 128 - n), F32)], axis=1)
    half = product((inverse_one, None), (high, low), n)
    gram_two = product(half, (turned, None), n)
    inverse_two = eliminate((gram_two[0] + gram_two[1]) * rest, n)
    both = lane_of(inverse_two, 0) * row_of(inverse_one, 0)
    for k in range(1, n):
        both = both + lane_of(inverse_two, k) * row_of(inverse_one, k)
    return both


def kernel(
    sizes,
    orb_ref,
    pot_ref,
    out_ref,
    e0,
    e1,
    e2,
    raw,
    diag,
    third,
    spread,
    grouped,
    wide,
    swap,
    table,
    split_x,
    back,
    gram_orb,
    gram_dom,
    load_sem,
    halo_send,
    halo_recv,
    pot_send,
    pot_recv,
    fwd_send,
    fwd_recv,
    gram_send,
    gram_recv,
    bck_send,
    bck_recv,
    all_send,
    all_recv,
    swap_send,
    swap_recv,
):
    doms, orbs, own, layers, ny, nz, cells = sizes
    n = own * orbs
    chunk = ny // orbs
    half = layers - 6
    pairs = orbs // 2
    d = lax.axis_index("dom")
    o = lax.axis_index("orb")
    left = lax.rem(d + doms - 1, doms)
    right = lax.rem(d + 1, doms)

    barrier = pltpu.get_barrier_semaphore()

    @pl.loop(1, orbs)
    def _(p):
        pl.semaphore_signal(
            barrier, inc=1, device_id={"orb": lax.rem(o + p, orbs)}, device_id_type=MESH
        )

    @pl.loop(1, doms)
    def _(p):
        pl.semaphore_signal(
            barrier, inc=1, device_id={"dom": lax.rem(d + p, doms)}, device_id_type=MESH
        )

    loads = [pltpu.make_async_copy(pot_ref, raw.at[pl.ds(6, layers)], load_sem.at[0])]
    for a in range(own):
        loads.append(pltpu.make_async_copy(orb_ref.at[a], e0.at[a, pl.ds(9, layers)], load_sem.at[1 + a]))
    for copy in loads:
        copy.start()

    pl.semaphore_wait(barrier, orbs - 1 + doms - 1)

    fields = (e0, e1, e2)

    def halo(a, begin, end):
        out = []
        for side, (at, to_at, to) in enumerate(
            ((layers - end, 9 - end, right), (begin, layers + 9 + begin, left))
        ):
            out.append(
                pltpu.make_async_remote_copy(
                    src_ref=orb_ref.at[a, pl.ds(at, end - begin)],
                    dst_ref=e0.at[a, pl.ds(to_at, end - begin)],
                    send_sem=halo_send.at[a, begin // 3 + begin // 8, side],
                    recv_sem=halo_recv.at[a, begin // 3 + begin // 8, side],
                    device_id={"dom": to},
                    device_id_type=MESH,
                )
            )
        return out

    mine = pl.ds(chunk * o, chunk)
    across = []
    for side, (at, to_at, to) in enumerate(((layers - 6, 0, right), (0, layers + 6, left))):
        across.append(
            pltpu.make_async_remote_copy(
                src_ref=pot_ref.at[pl.ds(at, 6), mine],
                dst_ref=raw.at[pl.ds(to_at, 6), mine],
                send_sem=pot_send.at[0, side],
                recv_sem=pot_recv.at[0, side],
                device_id={"dom": to},
                device_id_type=MESH,
            )
        )

    def share_margins():
        for side, at in enumerate((0, layers + 6)):

            @pl.loop(1, orbs)
            def _(p):
                pltpu.make_async_remote_copy(
                    src_ref=raw.at[pl.ds(at, 6), mine],
                    dst_ref=raw.at[pl.ds(at, 6), mine],
                    send_sem=pot_send.at[1, side],
                    recv_sem=pot_recv.at[1, side],
                    device_id={"orb": lax.rem(o + p, orbs)},
                    device_id_type=MESH,
                ).start()

    def wait_margins(sems):
        for side in range(2):
            block = raw.at[pl.ds(0, 6), pl.ds(0, ny - chunk)]
            pltpu.make_async_copy(block, block, sems.at[1, side]).wait()

    def start(copies):
        for copy in copies:
            copy.start()

    def wait(copies):
        for copy in copies:
            copy.wait()

    reach = [(0, 3), (3, 6), (6, 9)]
    pieces = [reach] * (own - 1) + [reach[:2] + [(6, 8), (8, 9)]]
    start(across)
    for a in range(own):
        for begin, end in pieces[a]:
            start(halo(a, begin, end))

    def apply_layer(stage, a, layer):
        src = fields[stage]
        at = layer + 9 - 3 * stage
        centre = src[a, at]
        result = diag[layer + 6] * centre
        for k in range(1, 4):
            near = src[a, at + k] + src[a, at - k]
            near = near + (pltpu.roll(centre, k, 0) + pltpu.roll(centre, ny - k, 0))
            near = near + (pltpu.roll(centre, k, 1) + pltpu.roll(centre, nz - k, 1))
            result = result + STEP[k] * near
        if stage > 0:
            result = 2.0 * result - fields[stage - 1][a, at + 3]
        if stage < 2:
            fields[stage + 1][a, at - 3] = result
        else:
            tiles = result.reshape(orbs, chunk, nz)
            slot = slot_layers.index(layer)
            third[:, a, slot] = tiles
            if slot < half:
                for q in range(2 * pairs - 1):
                    for parity in range(2):
                        spread[parity, q, a, slot] = tiles[2 * (q % pairs) + parity]

    inner = range(3, layers - 3)
    slot_layers = [*inner, 1, 2, layers - 3, layers - 2, 0, layers - 1]

    def newly(stage, a, begin, end):
        low, high = 3 * (stage + 1), layers - 3 * (stage + 1)
        for layer in (*range(low - end, low - begin), *range(high + begin, high + end)):
            apply_layer(stage, a, layer)

    slots_of = {(3, 6): ((0, half),), (6, 9): ((half, 6),), (6, 8): ((half, 4),), (8, 9): ((half + 4, 2),)}

    def to_cells(a, piece):
        part = pieces[a].index(piece) - 1
        for at, count in slots_of[piece]:

            @pl.loop(1, orbs)
            def _(p):
                to = lax.rem(o + p, orbs)
                pltpu.make_async_remote_copy(
                    src_ref=third.at[to, a, pl.ds(at, count)],
                    dst_ref=grouped.at[own * o + a, pl.ds(at, count)],
                    send_sem=fwd_send.at[a, part],
                    recv_sem=fwd_recv.at[a, part],
                    device_id={"orb": to},
                    device_id_type=MESH,
                ).start()

        for at, count in slots_of[piece]:
            for slot in range(at, at + count):
                grouped[own * o + a, slot] = third[o, a, slot]

    def wait_cells(a, part, sems):
        count = sum(count for _, count in slots_of[pieces[a][part + 1]])
        block = grouped.at[pl.ds(0, orbs - 1), pl.ds(0, count)]
        pltpu.make_async_copy(block, block, sems.at[a, part]).wait()

    def weigh(begin, end):
        @pl.loop(begin, end)
        def _(i):
            diag[i] = raw[i] * (1.0 / filter_half) + DIAGONAL

    wait(loads)
    weigh(6, layers + 6)
    for layer in inner:
        apply_layer(0, 0, layer)
    for copy in across:
        copy.wait()
    share_margins()
    for a in range(own):
        if a > 0:
            for layer in inner:
                apply_layer(0, a, layer)
        for begin, end in pieces[a]:
            wait(halo(a, begin, end))
            if a == 0 and begin == 3:
                wait_margins(pot_recv)
                weigh(0, 6)
                weigh(layers + 6, layers + 12)
            newly(0, a, begin, end)
            newly(1, a, begin, end)
            if begin > 0:
                newly(2, a, begin, end)
                to_cells(a, (begin, end))

    place, parity = o // 2, lax.rem(o, 2)
    other = o + 1 - 2 * parity

    def gather(a, at, count):
        @pl.loop(1, orbs)
        def _(p):
            to = lax.rem(o + p, orbs)
            pltpu.make_async_remote_copy(
                src_ref=spread.at[lax.rem(to, 2), pl.ds(to // 2 + 1, pairs - 1), a, pl.ds(at, count)],
                dst_ref=wide.at[:, own * o + a, pl.ds(at, count)],
                send_sem=all_send.at[0],
                recv_sem=all_recv.at[0],
                device_id={"orb": to},
                device_id_type=MESH,
            ).start()

    def gather_own():
        for k in range(1, pairs):
            for a in range(own):
                wide[k - 1, own * o + a] = spread[parity, place + k, a]

    def gather_rest():
        if EARLY < half:
            gather(0, EARLY, half - EARLY)
        for a in range(1, own):
            gather(a, 0, half)
        gather_own()

    def gather_wait(sem):
        block = wide.at[:, pl.ds(0, own * (orbs - 1))]
        pltpu.make_async_copy(block, block, sem.at[0]).wait()

    if EARLY:
        gather(0, 0, EARLY)

    flat = grouped.reshape(n * layers * chunk, nz)
    flat_back = back.reshape(n * 6 * chunk, nz)
    stride = layers * chunk

    def split_slots(ranges):
        def larger(slot, most):
            for r in range(chunk):
                most = jnp.maximum(most, jnp.abs(flat[pl.ds(slot * chunk + r, n, stride=stride), :]))
            return most

        most = jnp.zeros((n, nz), F32)
        for at, count in ranges:
            most = lax.fori_loop(at, at + count, larger, most, unroll=2)
        anchor = anchor_of(jnp.broadcast_to(jnp.max(most, axis=1, keepdims=True), (n, nz)))

        for at, count in ranges:

            @pl.loop(at, at + count, unroll=2)
            def _(slot):
                for r in range(chunk):
                    row = slot * chunk + r
                    x = flat[pl.ds(row, n, stride=stride), :]
                    lanes = pl.ds(pl.multiple_of(row * nz, nz), nz)
                    for part, value in enumerate(limbs(x, anchor)):
                        split_x[pl.ds(part * n, n), lanes] = value

    def gram_of(ranges, pair):
        for slot in (slot for at, count in ranges for slot in range(at, at + count)):
            x = split_x[:, slot * chunk * nz : (slot + 1) * chunk * nz]
            value = lax.dot_general(x, x, (((1,), (1,)), ((), ())), preferred_element_type=F32)
            if pair is None:
                pair = value, jnp.zeros_like(value)
            else:
                high, error = two_sum(pair[0], value)
                pair = high, pair[1] + error
        return pair

    lane = lax.broadcasted_iota(jnp.int32, (8, 128), 1)
    lane4 = lax.broadcasted_iota(jnp.int32, (4, 128), 1)
    lows = (lane4 & 32) == 32

    def total(pair):
        parts = [tuple(v[p * n : (p + 1) * n] for v in pair) for p in range(LIMBS)]
        low_first = add_pairs(add_pairs(parts[3], parts[2]), add_pairs(parts[1], parts[0]))
        pad = jnp.zeros((n, 128 - LIMBS * n), F32)
        wide = tuple(jnp.concatenate([v, pad], axis=1) for v in low_first)
        for step in (2 * n, n):
            wide = add_pairs(wide, tuple(pltpu.roll(v, 128 - step, 1) for v in wide))
        top, bottom = tuple(v[:8] for v in wide), tuple(pltpu.roll(v[8:], n, 1) for v in wide)
        high, low = (jnp.where(lane < n, t, b) for t, b in zip(top, bottom))
        packed = jnp.where(lane < 2 * n, high, pltpu.roll(low, 2 * n, 1))
        packed = jnp.where(lane4 < 64, packed[:4], pltpu.roll(packed, 64, 1)[4:])
        for which, (axis, count, me, buf) in enumerate((("orb", orbs, o, gram_orb), ("dom", doms, d, gram_dom))):
            buf[me] = packed

            @pl.loop(1, count)
            def _(p):
                pltpu.make_async_remote_copy(
                    src_ref=buf.at[me],
                    dst_ref=buf.at[me],
                    send_sem=gram_send.at[which],
                    recv_sem=gram_recv.at[which],
                    device_id={axis: lax.rem(me + p, count)},
                    device_id_type=MESH,
                ).start()

            if which == 0:
                gather_rest()
            block = buf.at[pl.ds(0, count - 1)]
            pltpu.make_async_copy(block, block, gram_recv.at[which]).wait()
            value, error = buf[...], None
            while count > 1:
                count //= 2
                value, extra = two_sum(value[:count], value[count:])
                error = extra if error is None else extra + (error[:count] + error[count:])
            packed = value[0] + jnp.where(lows, pltpu.roll(error[0], 2 * n, 1), 0.0)
        packed = jnp.concatenate([packed, pltpu.roll(packed, 64, 1)], axis=0)
        low = pltpu.roll(packed, 128 - 2 * n, 1)
        pair = tuple(
            jnp.where(
                lax.broadcasted_iota(jnp.int32, (n, 128), 1) < n,
                jnp.concatenate([v, pltpu.roll(v, 128 - n, 1)], axis=0),
                0.0,
            )
            for v in (packed, low)
        )
        return two_sum(pair[0], pair[1])

    def stacked(matrix):
        wide = matrix
        for part in range(1, LIMBS):
            wide = wide + pltpu.roll(matrix, part * n, 1)
        return jnp.concatenate(split3(wide), axis=0)[:, : LIMBS * n]

    def applied(weights, lanes):
        full = jnp.dot(weights, split_x[:, lanes], preferred_element_type=F32)
        return full[0:n] + (full[n : 2 * n] + full[2 * n : 3 * n])

    pair = None
    for part in range(3):
        for a in range(own):
            if part < len(pieces[a]) - 1:
                wait_cells(a, part, fwd_recv)
        ranges = slots_of[pieces[-1][part + 1]]
        split_slots(ranges)
        pair = gram_of(ranges, pair)
    gram = total(pair)
    matrix = combined(gram, float(cells), n)
    weights = stacked(matrix)

    parts = ((layers - 3, 3), (0, 3))
    for part, (layer, count) in enumerate(parts):
        for i in range(count):
            slot = slot_layers.index(layer + i)
            y = applied(weights, pl.ds(slot * chunk * nz, chunk * nz))
            for r in range(chunk):
                flat_back[pl.ds((part * 3 + i) * chunk + r, n, stride=6 * chunk), :] = y[:, r * nz : (r + 1) * nz]

        @pl.loop(1, orbs)
        def _(p):
            to = lax.rem(o + p, orbs)
            pltpu.make_async_remote_copy(
                src_ref=back.at[pl.ds(own * to, own), pl.ds(part * 3, count)],
                dst_ref=out_ref.at[:, pl.ds(layer, count), pl.ds(chunk * o, chunk)],
                send_sem=bck_send.at[part],
                recv_sem=bck_recv.at[part],
                device_id={"orb": to},
                device_id_type=MESH,
            ).start()

    all_rows = lax.broadcasted_iota(jnp.int32, (n, 128), 0)
    for i in range(2 * own):
        chosen = own * o + i if i < own else own * other + i - own
        row = jnp.sum(jnp.where(all_rows == chosen, matrix, 0.0), axis=0, keepdims=True)
        row = jnp.broadcast_to(row, (8, 128))
        for j in range(n):
            table[i, j] = lane_of(row, j)
    gather_wait(all_recv)

    def chunk_rows(k):
        return pl.ds(pl.multiple_of(chunk * (2 * lax.rem(place + k, pairs) + parity), chunk), chunk)

    @pl.loop(0, half)
    def _(slot):
        for k in range(pairs):
            x = [grouped[j, slot] if k == 0 else wide[k - 1, j, slot] for j in range(n)]
            for i in range(2 * own):
                terms = [table[i, j] * x[j] for j in range(n)]
                while len(terms) > 1:
                    terms = [p + q for p, q in zip(terms[::2], terms[1::2])]
                if i < own:
                    out_ref[i, slot + 3, chunk_rows(k), :] = terms[0]
                else:
                    swap[k, i - own, slot] = terms[0]

    for k in range(pairs):
        pltpu.make_async_remote_copy(
            src_ref=swap.at[k],
            dst_ref=out_ref.at[:, pl.ds(3, half), chunk_rows(k)],
            send_sem=swap_send.at[0],
            recv_sem=swap_recv.at[0],
            device_id={"orb": other},
            device_id_type=MESH,
        ).start()
    for a in range(own):
        for part, (layer, count) in enumerate(parts):
            out_ref[a, pl.ds(layer, count), pl.ds(pl.multiple_of(chunk * o, chunk), chunk), :] = back[
                own * o + a, pl.ds(part * 3, count)
            ]
    for sem in (swap_send, swap_recv):
        pltpu.make_async_copy(swap, swap, sem.at[0]).wait()
    for part, (layer, count) in enumerate(parts):
        block = back.at[pl.ds(0, own * (orbs - 1)), pl.ds(part * 3, count)]
        pltpu.make_async_copy(block, block, bck_send.at[part]).wait()
        pltpu.make_async_copy(block, block, bck_recv.at[part]).wait()
    gather_wait(all_send)
    wait_margins(pot_send)
    for a in range(own):
        for part in range(len(pieces[a]) - 1):
            wait_cells(a, part, fwd_send)
    for which, buf in enumerate((gram_orb, gram_dom)):
        block = buf.at[pl.ds(0, (orbs, doms)[which] - 1)]
        pltpu.make_async_copy(block, block, gram_send.at[which]).wait()


def on_device(orbitals, potential):
    own, layers, ny, nz = orbitals.shape
    doms, orbs = lax.axis_size("dom"), lax.axis_size("orb")
    n = own * orbs
    chunk = ny // orbs
    cells = layers * doms * ny * nz
    width = layers * chunk * nz
    dma = pltpu.SemaphoreType.DMA

    def field(extra):
        return pltpu.VMEM((own, layers + extra, ny, nz), F32)

    return pl.pallas_call(
        functools.partial(kernel, (doms, orbs, own, layers, ny, nz, cells)),
        out_shape=pltpu.VMEM(orbitals.shape, F32),
        in_specs=[pl.BlockSpec(memory_space=pltpu.HBM)] * 2,
        out_specs=pl.BlockSpec(memory_space=pltpu.VMEM),
        scratch_shapes=[
            field(18),
            field(12),
            field(6),
            pltpu.VMEM((layers + 12, ny, nz), F32),
            pltpu.VMEM((layers + 12, ny, nz), F32),
            pltpu.VMEM((orbs, own, layers, chunk, nz), F32),
            pltpu.VMEM((2, orbs - 1, own, layers - 6, chunk, nz), F32),
            pltpu.VMEM((n, layers, chunk, nz), F32),
            pltpu.VMEM((orbs // 2 - 1, n, layers - 6, chunk, nz), F32),
            pltpu.VMEM((orbs // 2, own, layers - 6, chunk, nz), F32),
            pltpu.VMEM((2 * own, n, 8, 128), F32),
            pltpu.VMEM((LIMBS * n, width), BF16),
            pltpu.VMEM((n, 6, chunk, nz), F32),
            pltpu.VMEM((orbs, 4, 128), F32),
            pltpu.VMEM((doms, 4, 128), F32),
            dma((1 + own,)),
            dma((own, 4, 2)),
            dma((own, 4, 2)),
            dma((2, 2)),
            dma((2, 2)),
            dma((own, 3)),
            dma((own, 3)),
            dma((2,)),
            dma((2,)),
            dma((2,)),
            dma((2,)),
            dma((1,)),
            dma((1,)),
            dma((1,)),
            dma((1,)),
        ],
        compiler_params=pltpu.CompilerParams(
            collective_id=0, has_side_effects=True, vmem_limit_bytes=40 * 1024 * 1024
        ),
        cost_estimate=pl.CostEstimate(flops=100_000_000, bytes_accessed=4_000_000, transcendentals=0),
    )(*(pltpu.with_memory_space_constraint(v, pltpu.HBM) for v in (orbitals, potential)))


def solution(mesh):
    return jax.shard_map(
        on_device,
        mesh=mesh,
        in_specs=(P("orb", "dom", None, None), P("dom", None, None)),
        out_specs=P("orb", "dom", None, None),
        check_vma=False,
    )
```

```python
import functools

import jax
import jax.numpy as jnp
from jax import lax
from jax.experimental import pallas as pl
from jax.experimental.pallas import tpu as pltpu
from jax.sharding import PartitionSpec as P

MESH = pl.DeviceIdType.MESH
F32 = jnp.float32
BF16 = jnp.bfloat16
coefficients = (-49.0 / 18.0, 1.5, -0.15, 1.0 / 90.0)
spacing = 0.5
filter_centre = 23.0
filter_half = 23.0
kinetic = -0.5 / (spacing * spacing) / filter_half
STEP = tuple(kinetic * c for c in coefficients)
DIAGONAL = 3.0 * STEP[0] - filter_centre / filter_half
LIMBS = 4
GATHERED = 6


def split3(x):
    hi = x.astype(BF16)
    rest = x - hi.astype(F32)
    mid = rest.astype(BF16)
    low = (rest - mid.astype(F32)).astype(BF16)
    return hi, mid, low


def anchor_of(largest):
    shift = largest * 2.0**23
    return ((largest + shift) - shift) * (1.25 * 2.0**17)


def limbs(x, anchor):
    out = []
    for part in range(LIMBS):
        place = anchor * 2.0 ** (-8 * part)
        value = (x + place) - place
        x = x - value
        out.append(value.astype(BF16))
    return out


def two_sum(a, b):
    total = a + b
    part = total - a
    return total, (a - (total - part)) + (b - part)


def add_pairs(a, b):
    total, error = two_sum(a[0], b[0])
    return total, error + (a[1] + b[1])


def halves(x):
    wide = x * 4097.0
    high = wide - (wide - x)
    return high, x - high


def lane_of(x, j):
    return jnp.broadcast_to(x[:, j : j + 1], x.shape)


def row_of(x, j):
    return jnp.broadcast_to(x[j : j + 1, :], x.shape)


def product(left, right, n):
    left_high, left_low = halves(left[0])
    right_high, right_low = halves(right[0])
    total, low = None, None
    for k in range(n):
        a, ah, al = lane_of(left[0], k), lane_of(left_high, k), lane_of(left_low, k)
        b, bh, bl = row_of(right[0], k), row_of(right_high, k), row_of(right_low, k)
        value = a * b
        error = ((ah * bh - value) + ah * bl + al * bh) + al * bl
        if right[1] is not None:
            error = error + a * row_of(right[1], k)
        if left[1] is not None:
            error = error + lane_of(left[1], k) * b
        if total is None:
            total, low = value, error
        else:
            total, carry = two_sum(total, value)
            low = low + (carry + error)
    return total, low


def eliminate(gram, n):
    rows = lax.broadcasted_iota(jnp.int32, (n, 128), 0)
    lanes = lax.broadcasted_iota(jnp.int32, (n, 128), 1)
    work = jnp.where(lanes < n, gram, 0.0) + jnp.where(lanes == rows + n, 1.0, 0.0)
    for j in range(0, n, 2):
        first, second = lane_of(work, j), lane_of(work, j + 1)
        row, next_row = row_of(work, j), row_of(work, j + 1)
        a, b, c, d = row_of(first, j), row_of(second, j), row_of(first, j + 1), row_of(second, j + 1)
        over = 1.0 / a
        over_next = a / (a * d - b * c)
        factor = first * over
        next_factor = jnp.where(rows > j + 1, (second - factor * b) * over_next, 0.0)
        next_row = next_row - (c * over) * row
        work = work - jnp.where(rows > j, factor, 0.0) * row - next_factor * next_row
    diagonal = jnp.sum(jnp.where(lanes == rows, work, 0.0), axis=1, keepdims=True)
    scaled = work / jnp.sqrt(jnp.broadcast_to(diagonal, (n, 128)))
    return jnp.where(lanes < n, pltpu.roll(scaled, 128 - n, 1), 0.0)


def combined(gram, cells, n):
    scale = 2.0**-20
    high, low = gram[0] * scale, gram[1] * scale
    rest = 1.0 / (cells * scale)
    inverse_one = eliminate(high * rest, n)
    turned = jnp.transpose(inverse_one)[:n]
    turned = jnp.concatenate([turned, jnp.zeros((n, 128 - n), F32)], axis=1)
    half = product((inverse_one, None), (high, low), n)
    gram_two = product(half, (turned, None), n)
    inverse_two = eliminate((gram_two[0] + gram_two[1]) * rest, n)
    both = lane_of(inverse_two, 0) * row_of(inverse_one, 0)
    for k in range(1, n):
        both = both + lane_of(inverse_two, k) * row_of(inverse_one, k)
    return both


def kernel(
    sizes,
    orb_ref,
    pot_ref,
    out_ref,
    e0,
    e1,
    e2,
    raw,
    diag,
    third,
    spread,
    grouped,
    wide,
    swap,
    table,
    split_x,
    back,
    gram_orb,
    gram_dom,
    load_sem,
    halo_send,
    halo_recv,
    pot_send,
    pot_recv,
    fwd_send,
    fwd_recv,
    gram_send,
    gram_recv,
    bck_send,
    bck_recv,
    all_send,
    all_recv,
    swap_send,
    swap_recv,
):
    doms, orbs, own, layers, ny, nz, cells = sizes
    n = own * orbs
    chunk = ny // orbs
    half = layers - 6
    pairs = orbs // 2
    d = lax.axis_index("dom")
    o = lax.axis_index("orb")
    left = lax.rem(d + doms - 1, doms)
    right = lax.rem(d + 1, doms)

    barrier = pltpu.get_barrier_semaphore()

    @pl.loop(1, orbs)
    def _(p):
        pl.semaphore_signal(
            barrier, inc=1, device_id={"orb": lax.rem(o + p, orbs)}, device_id_type=MESH
        )

    @pl.loop(1, doms)
    def _(p):
        pl.semaphore_signal(
            barrier, inc=1, device_id={"dom": lax.rem(d + p, doms)}, device_id_type=MESH
        )

    loads = [pltpu.make_async_copy(pot_ref, raw.at[pl.ds(6, layers)], load_sem.at[0])]
    for a in range(own):
        loads.append(pltpu.make_async_copy(orb_ref.at[a], e0.at[a, pl.ds(9, layers)], load_sem.at[1 + a]))
    for copy in loads:
        copy.start()

    pl.semaphore_wait(barrier, orbs - 1 + doms - 1)

    fields = (e0, e1, e2)

    def halo(a, begin, end):
        out = []
        for side, (at, to_at, to) in enumerate(
            ((layers - end, 9 - end, right), (begin, layers + 9 + begin, left))
        ):
            out.append(
                pltpu.make_async_remote_copy(
                    src_ref=orb_ref.at[a, pl.ds(at, end - begin)],
                    dst_ref=e0.at[a, pl.ds(to_at, end - begin)],
                    send_sem=halo_send.at[a, begin // 3 + begin // 8, side],
                    recv_sem=halo_recv.at[a, begin // 3 + begin // 8, side],
                    device_id={"dom": to},
                    device_id_type=MESH,
                )
            )
        return out

    mine = pl.ds(chunk * o, chunk)
    across = []
    for side, (at, to_at, to) in enumerate(((layers - 6, 0, right), (0, layers + 6, left))):
        across.append(
            pltpu.make_async_remote_copy(
                src_ref=pot_ref.at[pl.ds(at, 6), mine],
                dst_ref=raw.at[pl.ds(to_at, 6), mine],
                send_sem=pot_send.at[0, side],
                recv_sem=pot_recv.at[0, side],
                device_id={"dom": to},
                device_id_type=MESH,
            )
        )

    def share_margins():
        for side, at in enumerate((0, layers + 6)):

            @pl.loop(1, orbs)
            def _(p):
                pltpu.make_async_remote_copy(
                    src_ref=raw.at[pl.ds(at, 6), mine],
                    dst_ref=raw.at[pl.ds(at, 6), mine],
                    send_sem=pot_send.at[1, side],
                    recv_sem=pot_recv.at[1, side],
                    device_id={"orb": lax.rem(o + p, orbs)},
                    device_id_type=MESH,
                ).start()

    def wait_margins(sems):
        for side in range(2):
            block = raw.at[pl.ds(0, 6), pl.ds(0, ny - chunk)]
            pltpu.make_async_copy(block, block, sems.at[1, side]).wait()

    def start(copies):
        for copy in copies:
            copy.start()

    def wait(copies):
        for copy in copies:
            copy.wait()

    reach = [(0, 3), (3, 6), (6, 9)]
    pieces = [reach] * (own - 1) + [reach[:2] + [(6, 8), (8, 9)]]
    start(across)
    for a in range(own):
        for begin, end in pieces[a]:
            start(halo(a, begin, end))

    def apply_layer(stage, a, layer):
        src = fields[stage]
        at = layer + 9 - 3 * stage
        centre = src[a, at]
        result = diag[layer + 6] * centre
        for k in range(1, 4):
            near = src[a, at + k] + src[a, at - k]
            near = near + (pltpu.roll(centre, k, 0) + pltpu.roll(centre, ny - k, 0))
            near = near + (pltpu.roll(centre, k, 1) + pltpu.roll(centre, nz - k, 1))
            result = result + STEP[k] * near
        if stage > 0:
            result = 2.0 * result - fields[stage - 1][a, at + 3]
        if stage < 2:
            fields[stage + 1][a, at - 3] = result
        else:
            tiles = result.reshape(orbs, chunk, nz)
            slot = slot_layers.index(layer)
            third[:, a, slot] = tiles
            if slot < GATHERED:
                for q in range(2 * pairs - 1):
                    for parity in range(2):
                        spread[parity, q, a, slot] = tiles[2 * (q % pairs) + parity]

    inner = range(3, layers - 3)
    slot_layers = [*inner, 1, 2, layers - 3, layers - 2, 0, layers - 1]

    def newly(stage, a, begin, end):
        low, high = 3 * (stage + 1), layers - 3 * (stage + 1)
        for layer in (*range(low - end, low - begin), *range(high + begin, high + end)):
            apply_layer(stage, a, layer)

    slots_of = {(3, 6): ((0, half),), (6, 9): ((half, 6),), (6, 8): ((half, 4),), (8, 9): ((half + 4, 2),)}

    def to_cells(a, piece):
        part = pieces[a].index(piece) - 1
        for at, count in slots_of[piece]:

            @pl.loop(1, orbs)
            def _(p):
                to = lax.rem(o + 1 + lax.rem(p + 2, orbs - 1), orbs)
                pltpu.make_async_remote_copy(
                    src_ref=third.at[to, a, pl.ds(at, count)],
                    dst_ref=grouped.at[own * o + a, pl.ds(at, count)],
                    send_sem=fwd_send.at[a, part],
                    recv_sem=fwd_recv.at[a, part],
                    device_id={"orb": to},
                    device_id_type=MESH,
                ).start()

        for at, count in slots_of[piece]:
            for slot in range(at, at + count):
                grouped[own * o + a, slot] = third[o, a, slot]

    def wait_cells(a, part, sems):
        count = sum(count for _, count in slots_of[pieces[a][part + 1]])
        block = grouped.at[pl.ds(0, orbs - 1), pl.ds(0, count)]
        pltpu.make_async_copy(block, block, sems.at[a, part]).wait()

    def weigh(begin, end):
        @pl.loop(begin, end)
        def _(i):
            diag[i] = raw[i] * (1.0 / filter_half) + DIAGONAL

    wait(loads)
    weigh(6, layers + 6)
    for layer in inner:
        apply_layer(0, 0, layer)
    for copy in across:
        copy.wait()
    share_margins()
    for a in range(own):
        if a > 0:
            for layer in inner:
                apply_layer(0, a, layer)
        for begin, end in pieces[a]:
            wait(halo(a, begin, end))
            if a == 0 and begin == 3:
                wait_margins(pot_recv)
                weigh(0, 6)
                weigh(layers + 6, layers + 12)
            newly(0, a, begin, end)
            newly(1, a, begin, end)
            if begin > 0:
                newly(2, a, begin, end)
                to_cells(a, (begin, end))

    place, parity = o // 2, lax.rem(o, 2)
    other = o + 1 - 2 * parity

    def gather(a):
        @pl.loop(1, orbs)
        def _(p):
            to = lax.rem(o + 1 + lax.rem(p + 2, orbs - 1), orbs)
            pltpu.make_async_remote_copy(
                src_ref=spread.at[lax.rem(to, 2), pl.ds(to // 2 + 1, pairs - 1), a],
                dst_ref=wide.at[:, own * o + a],
                send_sem=all_send.at[0],
                recv_sem=all_recv.at[0],
                device_id={"orb": to},
                device_id_type=MESH,
            ).start()

    def gather_own():
        for k in range(1, pairs):
            for a in range(own):
                wide[k - 1, own * o + a] = spread[parity, place + k, a]

    def gather_rest():
        for a in range(own):
            gather(a)
        gather_own()

    def gather_wait(sem):
        block = wide.at[:, pl.ds(0, own * (orbs - 1))]
        pltpu.make_async_copy(block, block, sem.at[0]).wait()

    flat = grouped.reshape(n * layers * chunk, nz)
    flat_back = back.reshape(n * (layers - GATHERED) * chunk, nz)
    stride = layers * chunk

    def split_slots(ranges):
        def larger(slot, most):
            for r in range(chunk):
                most = jnp.maximum(most, jnp.abs(flat[pl.ds(slot * chunk + r, n, stride=stride), :]))
            return most

        most = jnp.zeros((n, nz), F32)
        for at, count in ranges:
            most = lax.fori_loop(at, at + count, larger, most, unroll=2)
        anchor = anchor_of(jnp.broadcast_to(jnp.max(most, axis=1, keepdims=True), (n, nz)))

        for at, count in ranges:

            @pl.loop(at, at + count, unroll=2)
            def _(slot):
                for r in range(chunk):
                    row = slot * chunk + r
                    x = flat[pl.ds(row, n, stride=stride), :]
                    lanes = pl.ds(pl.multiple_of(row * nz, nz), nz)
                    for part, value in enumerate(limbs(x, anchor)):
                        split_x[pl.ds(part * n, n), lanes] = value

    def gram_of(ranges, pair):
        for slot in (slot for at, count in ranges for slot in range(at, at + count)):
            x = split_x[:, slot * chunk * nz : (slot + 1) * chunk * nz]
            value = lax.dot_general(x, x, (((1,), (1,)), ((), ())), preferred_element_type=F32)
            if pair is None:
                pair = value, jnp.zeros_like(value)
            else:
                high, error = two_sum(pair[0], value)
                pair = high, pair[1] + error
        return pair

    lane = lax.broadcasted_iota(jnp.int32, (8, 128), 1)
    lane4 = lax.broadcasted_iota(jnp.int32, (4, 128), 1)
    lows = (lane4 & 32) == 32

    def total(pair):
        parts = [tuple(v[p * n : (p + 1) * n] for v in pair) for p in range(LIMBS)]
        low_first = add_pairs(add_pairs(parts[3], parts[2]), add_pairs(parts[1], parts[0]))
        pad = jnp.zeros((n, 128 - LIMBS * n), F32)
        wide = tuple(jnp.concatenate([v, pad], axis=1) for v in low_first)
        for step in (2 * n, n):
            wide = add_pairs(wide, tuple(pltpu.roll(v, 128 - step, 1) for v in wide))
        top, bottom = tuple(v[:8] for v in wide), tuple(pltpu.roll(v[8:], n, 1) for v in wide)
        high, low = (jnp.where(lane < n, t, b) for t, b in zip(top, bottom))
        packed = jnp.where(lane < 2 * n, high, pltpu.roll(low, 2 * n, 1))
        packed = jnp.where(lane4 < 64, packed[:4], pltpu.roll(packed, 64, 1)[4:])
        for which, (axis, count, me, buf) in enumerate((("orb", orbs, o, gram_orb), ("dom", doms, d, gram_dom))):
            buf[me] = packed

            @pl.loop(1, count)
            def _(p):
                pltpu.make_async_remote_copy(
                    src_ref=buf.at[me],
                    dst_ref=buf.at[me],
                    send_sem=gram_send.at[which],
                    recv_sem=gram_recv.at[which],
                    device_id={axis: lax.rem(me + 1 + lax.rem(p + count // 2 - 2, count - 1), count)},
                    device_id_type=MESH,
                ).start()

            if which == 0:
                gather_rest()
            block = buf.at[pl.ds(0, count - 1)]
            pltpu.make_async_copy(block, block, gram_recv.at[which]).wait()
            value, error = buf[...], None
            while count > 1:
                count //= 2
                value, extra = two_sum(value[:count], value[count:])
                error = extra if error is None else extra + (error[:count] + error[count:])
            packed = value[0] + jnp.where(lows, pltpu.roll(error[0], 2 * n, 1), 0.0)
        packed = jnp.concatenate([packed, pltpu.roll(packed, 64, 1)], axis=0)
        low = pltpu.roll(packed, 128 - 2 * n, 1)
        pair = tuple(
            jnp.where(
                lax.broadcasted_iota(jnp.int32, (n, 128), 1) < n,
                jnp.concatenate([v, pltpu.roll(v, 128 - n, 1)], axis=0),
                0.0,
            )
            for v in (packed, low)
        )
        return two_sum(pair[0], pair[1])

    def stacked(matrix):
        wide = matrix
        for part in range(1, LIMBS):
            wide = wide + pltpu.roll(matrix, part * n, 1)
        return jnp.concatenate(split3(wide), axis=0)[:, : LIMBS * n]

    def applied(weights, lanes):
        full = jnp.dot(weights, split_x[:, lanes], preferred_element_type=F32)
        return full[0:n] + (full[n : 2 * n] + full[2 * n : 3 * n])

    pair = None
    for part in range(3):
        for a in range(own):
            if part < len(pieces[a]) - 1:
                wait_cells(a, part, fwd_recv)
        ranges = slots_of[pieces[-1][part + 1]]
        split_slots(ranges)
        pair = gram_of(ranges, pair)
    gram = total(pair)
    matrix = combined(gram, float(cells), n)
    weights = stacked(matrix)

    parts = ((3 + GATHERED, layers - 3 - GATHERED, 0), (0, 3, layers - 3 - GATHERED))
    for part, (layer, count, at) in enumerate(parts):
        for i in range(count):
            slot = slot_layers.index(layer + i)
            y = applied(weights, pl.ds(slot * chunk * nz, chunk * nz))
            for r in range(chunk):
                flat_back[pl.ds((at + i) * chunk + r, n, stride=(layers - GATHERED) * chunk), :] = y[:, r * nz : (r + 1) * nz]

        @pl.loop(1, orbs)
        def _(p):
            to = lax.rem(o + 1 + lax.rem(p + 2, orbs - 1), orbs)
            pltpu.make_async_remote_copy(
                src_ref=back.at[pl.ds(own * to, own), pl.ds(at, count)],
                dst_ref=out_ref.at[:, pl.ds(layer, count), pl.ds(chunk * o, chunk)],
                send_sem=bck_send.at[part],
                recv_sem=bck_recv.at[part],
                device_id={"orb": to},
                device_id_type=MESH,
            ).start()

    all_rows = lax.broadcasted_iota(jnp.int32, (n, 128), 0)
    for i in range(2 * own):
        chosen = own * o + i if i < own else own * other + i - own
        row = jnp.sum(jnp.where(all_rows == chosen, matrix, 0.0), axis=0, keepdims=True)
        row = jnp.broadcast_to(row, (8, 128))
        for j in range(n):
            table[i, j] = lane_of(row, j)
    gather_wait(all_recv)

    def chunk_rows(k):
        return pl.ds(pl.multiple_of(chunk * (2 * lax.rem(place + k, pairs) + parity), chunk), chunk)

    @pl.loop(0, GATHERED)
    def _(slot):
        for k in range(pairs):
            x = [grouped[j, slot] if k == 0 else wide[k - 1, j, slot] for j in range(n)]
            for i in range(2 * own):
                terms = [table[i, j] * x[j] for j in range(n)]
                while len(terms) > 1:
                    terms = [p + q for p, q in zip(terms[::2], terms[1::2])]
                if i < own:
                    out_ref[i, slot + 3, chunk_rows(k), :] = terms[0]
                else:
                    swap[k, i - own, slot] = terms[0]

    for k in range(pairs):
        pltpu.make_async_remote_copy(
            src_ref=swap.at[k],
            dst_ref=out_ref.at[:, pl.ds(3, GATHERED), chunk_rows(k)],
            send_sem=swap_send.at[0],
            recv_sem=swap_recv.at[0],
            device_id={"orb": other},
            device_id_type=MESH,
        ).start()
    for a in range(own):
        for layer, count, at in parts:
            out_ref[a, pl.ds(layer, count), pl.ds(pl.multiple_of(chunk * o, chunk), chunk), :] = back[
                own * o + a, pl.ds(at, count)
            ]
    for sem in (swap_send, swap_recv):
        pltpu.make_async_copy(swap, swap, sem.at[0]).wait()
    for part, (_, count, at) in enumerate(parts):
        block = back.at[pl.ds(0, own * (orbs - 1)), pl.ds(at, count)]
        pltpu.make_async_copy(block, block, bck_send.at[part]).wait()
        pltpu.make_async_copy(block, block, bck_recv.at[part]).wait()
    gather_wait(all_send)
    wait_margins(pot_send)
    for a in range(own):
        for part in range(len(pieces[a]) - 1):
            wait_cells(a, part, fwd_send)
    for which, buf in enumerate((gram_orb, gram_dom)):
        block = buf.at[pl.ds(0, (orbs, doms)[which] - 1)]
        pltpu.make_async_copy(block, block, gram_send.at[which]).wait()


def on_device(orbitals, potential):
    own, layers, ny, nz = orbitals.shape
    doms, orbs = lax.axis_size("dom"), lax.axis_size("orb")
    n = own * orbs
    chunk = ny // orbs
    cells = layers * doms * ny * nz
    width = layers * chunk * nz
    dma = pltpu.SemaphoreType.DMA

    def field(extra):
        return pltpu.VMEM((own, layers + extra, ny, nz), F32)

    return pl.pallas_call(
        functools.partial(kernel, (doms, orbs, own, layers, ny, nz, cells)),
        out_shape=pltpu.VMEM(orbitals.shape, F32),
        in_specs=[pl.BlockSpec(memory_space=pltpu.HBM)] * 2,
        out_specs=pl.BlockSpec(memory_space=pltpu.VMEM),
        scratch_shapes=[
            field(18),
            field(12),
            field(6),
            pltpu.VMEM((layers + 12, ny, nz), F32),
            pltpu.VMEM((layers + 12, ny, nz), F32),
            pltpu.VMEM((orbs, own, layers, chunk, nz), F32),
            pltpu.VMEM((2, orbs - 1, own, GATHERED, chunk, nz), F32),
            pltpu.VMEM((n, layers, chunk, nz), F32),
            pltpu.VMEM((orbs // 2 - 1, n, GATHERED, chunk, nz), F32),
            pltpu.VMEM((orbs // 2, own, GATHERED, chunk, nz), F32),
            pltpu.VMEM((2 * own, n, 8, 128), F32),
            pltpu.VMEM((LIMBS * n, width), BF16),
            pltpu.VMEM((n, layers - GATHERED, chunk, nz), F32),
            pltpu.VMEM((orbs, 4, 128), F32),
            pltpu.VMEM((doms, 4, 128), F32),
            dma((1 + own,)),
            dma((own, 4, 2)),
            dma((own, 4, 2)),
            dma((2, 2)),
            dma((2, 2)),
            dma((own, 3)),
            dma((own, 3)),
            dma((2,)),
            dma((2,)),
            dma((2,)),
            dma((2,)),
            dma((1,)),
            dma((1,)),
            dma((1,)),
            dma((1,)),
        ],
        compiler_params=pltpu.CompilerParams(
            collective_id=0, has_side_effects=True, vmem_limit_bytes=40 * 1024 * 1024
        ),
        cost_estimate=pl.CostEstimate(flops=100_000_000, bytes_accessed=4_000_000, transcendentals=0),
    )(*(pltpu.with_memory_space_constraint(v, pltpu.HBM) for v in (orbitals, potential)))


def solution(mesh):
    return jax.shard_map(
        on_device,
        mesh=mesh,
        in_specs=(P("orb", "dom", None, None), P("dom", None, None)),
        out_specs=P("orb", "dom", None, None),
        check_vma=False,
    )
```

```python
import functools

import jax
import jax.numpy as jnp
from jax import lax
from jax.experimental import pallas as pl
from jax.experimental.pallas import tpu as pltpu
from jax.sharding import PartitionSpec as P

MESH = pl.DeviceIdType.MESH
F32 = jnp.float32
BF16 = jnp.bfloat16
coefficients = (-49.0 / 18.0, 1.5, -0.15, 1.0 / 90.0)
spacing = 0.5
filter_centre = 23.0
filter_half = 23.0
kinetic = -0.5 / (spacing * spacing) / filter_half
STEP = tuple(kinetic * c for c in coefficients)
DIAGONAL = 3.0 * STEP[0] - filter_centre / filter_half
LIMBS = 4
GATHERED = 6


def split3(x):
    hi = x.astype(BF16)
    rest = x - hi.astype(F32)
    mid = rest.astype(BF16)
    low = (rest - mid.astype(F32)).astype(BF16)
    return hi, mid, low


def anchor_of(largest):
    shift = largest * 2.0**23
    return ((largest + shift) - shift) * (1.25 * 2.0**17)


def limbs(x, anchor):
    out = []
    for part in range(LIMBS):
        place = anchor * 2.0 ** (-8 * part)
        value = (x + place) - place
        x = x - value
        out.append(value.astype(BF16))
    return out


def two_sum(a, b):
    total = a + b
    part = total - a
    return total, (a - (total - part)) + (b - part)


def add_pairs(a, b):
    total, error = two_sum(a[0], b[0])
    return total, error + (a[1] + b[1])


def halves(x):
    wide = x * 4097.0
    high = wide - (wide - x)
    return high, x - high


def lane_of(x, j):
    return jnp.broadcast_to(x[:, j : j + 1], x.shape)


def row_of(x, j):
    return jnp.broadcast_to(x[j : j + 1, :], x.shape)


def product(left, right, n):
    left_high, left_low = halves(left[0])
    right_high, right_low = halves(right[0])
    total, low = None, None
    for k in range(n):
        a, ah, al = lane_of(left[0], k), lane_of(left_high, k), lane_of(left_low, k)
        b, bh, bl = row_of(right[0], k), row_of(right_high, k), row_of(right_low, k)
        value = a * b
        error = ((ah * bh - value) + ah * bl + al * bh) + al * bl
        if right[1] is not None:
            error = error + a * row_of(right[1], k)
        if left[1] is not None:
            error = error + lane_of(left[1], k) * b
        if total is None:
            total, low = value, error
        else:
            total, carry = two_sum(total, value)
            low = low + (carry + error)
    return total, low


def eliminate(gram, n):
    rows = lax.broadcasted_iota(jnp.int32, (n, 128), 0)
    lanes = lax.broadcasted_iota(jnp.int32, (n, 128), 1)
    work = jnp.where(lanes < n, gram, 0.0) + jnp.where(lanes == rows + n, 1.0, 0.0)
    for j in range(0, n, 2):
        first, second = lane_of(work, j), lane_of(work, j + 1)
        row, next_row = row_of(work, j), row_of(work, j + 1)
        a, b, c, d = row_of(first, j), row_of(second, j), row_of(first, j + 1), row_of(second, j + 1)
        over = 1.0 / a
        over_next = a / (a * d - b * c)
        factor = first * over
        next_factor = jnp.where(rows > j + 1, (second - factor * b) * over_next, 0.0)
        next_row = next_row - (c * over) * row
        work = work - jnp.where(rows > j, factor, 0.0) * row - next_factor * next_row
    diagonal = jnp.sum(jnp.where(lanes == rows, work, 0.0), axis=1, keepdims=True)
    scaled = work / jnp.sqrt(jnp.broadcast_to(diagonal, (n, 128)))
    return jnp.where(lanes < n, pltpu.roll(scaled, 128 - n, 1), 0.0)


def combined(gram, cells, n):
    scale = 2.0**-20
    high, low = gram[0] * scale, gram[1] * scale
    rest = 1.0 / (cells * scale)
    inverse_one = eliminate(high * rest, n)
    turned = jnp.transpose(inverse_one)[:n]
    turned = jnp.concatenate([turned, jnp.zeros((n, 128 - n), F32)], axis=1)
    half = product((inverse_one, None), (high, low), n)
    gram_two = product(half, (turned, None), n)
    inverse_two = eliminate((gram_two[0] + gram_two[1]) * rest, n)
    both = lane_of(inverse_two, 0) * row_of(inverse_one, 0)
    for k in range(1, n):
        both = both + lane_of(inverse_two, k) * row_of(inverse_one, k)
    return both


def kernel(
    sizes,
    orb_ref,
    pot_ref,
    out_ref,
    e0,
    e1,
    e2,
    raw,
    diag,
    third,
    spread,
    grouped,
    wide,
    swap,
    table,
    split_x,
    back,
    gram_orb,
    gram_dom,
    load_sem,
    halo_send,
    halo_recv,
    pot_send,
    pot_recv,
    fwd_send,
    fwd_recv,
    gram_send,
    gram_recv,
    bck_send,
    bck_recv,
    all_send,
    all_recv,
    swap_send,
    swap_recv,
):
    doms, orbs, own, layers, ny, nz, cells = sizes
    n = own * orbs
    chunk = ny // orbs
    half = layers - 6
    pairs = orbs // 2
    d = lax.axis_index("dom")
    o = lax.axis_index("orb")
    left = lax.rem(d + doms - 1, doms)
    right = lax.rem(d + 1, doms)

    barrier = pltpu.get_barrier_semaphore()

    near, far = 2 * orbs, doms // 2
    parity_d = lax.rem(d, 2)
    place_near = parity_d * orbs + o

    def near_device(p):
        to = lax.rem(place_near + p, near)
        return {"dom": d - parity_d + to // orbs, "orb": lax.rem(to, orbs)}

    def far_device(p):
        return {"dom": 2 * lax.rem(d // 2 + p, far) + parity_d}

    for neighbour in (left, right):
        pl.semaphore_signal(barrier, inc=1, device_id={"dom": neighbour}, device_id_type=MESH)

    @pl.loop(1, far)
    def _(p):
        pl.semaphore_signal(barrier, inc=1, device_id=far_device(p), device_id_type=MESH)

    @pl.loop(1, near)
    def _(p):
        pl.semaphore_signal(barrier, inc=1, device_id=near_device(p), device_id_type=MESH)

    loads = [pltpu.make_async_copy(pot_ref, raw.at[pl.ds(6, layers)], load_sem.at[0])]
    for a in range(own):
        loads.append(pltpu.make_async_copy(orb_ref.at[a], e0.at[a, pl.ds(9, layers)], load_sem.at[1 + a]))
    for copy in loads:
        copy.start()

    pl.semaphore_wait(barrier, 2 + near - 1 + far - 1)

    fields = (e0, e1, e2)

    def halo(a, begin, end):
        out = []
        for side, (at, to_at, to) in enumerate(
            ((layers - end, 9 - end, right), (begin, layers + 9 + begin, left))
        ):
            out.append(
                pltpu.make_async_remote_copy(
                    src_ref=orb_ref.at[a, pl.ds(at, end - begin)],
                    dst_ref=e0.at[a, pl.ds(to_at, end - begin)],
                    send_sem=halo_send.at[a, begin // 3 + begin // 8, side],
                    recv_sem=halo_recv.at[a, begin // 3 + begin // 8, side],
                    device_id={"dom": to},
                    device_id_type=MESH,
                )
            )
        return out

    mine = pl.ds(chunk * o, chunk)
    across = []
    for side, (at, to_at, to) in enumerate(((layers - 6, 0, right), (0, layers + 6, left))):
        across.append(
            pltpu.make_async_remote_copy(
                src_ref=pot_ref.at[pl.ds(at, 6), mine],
                dst_ref=raw.at[pl.ds(to_at, 6), mine],
                send_sem=pot_send.at[0, side],
                recv_sem=pot_recv.at[0, side],
                device_id={"dom": to},
                device_id_type=MESH,
            )
        )

    def share_margins():
        for side, at in enumerate((0, layers + 6)):

            @pl.loop(1, orbs)
            def _(p):
                pltpu.make_async_remote_copy(
                    src_ref=raw.at[pl.ds(at, 6), mine],
                    dst_ref=raw.at[pl.ds(at, 6), mine],
                    send_sem=pot_send.at[1, side],
                    recv_sem=pot_recv.at[1, side],
                    device_id={"orb": lax.rem(o + p, orbs)},
                    device_id_type=MESH,
                ).start()

    def wait_margins(sems):
        for side in range(2):
            block = raw.at[pl.ds(0, 6), pl.ds(0, ny - chunk)]
            pltpu.make_async_copy(block, block, sems.at[1, side]).wait()

    def start(copies):
        for copy in copies:
            copy.start()

    def wait(copies):
        for copy in copies:
            copy.wait()

    reach = [(0, 3), (3, 6), (6, 9)]
    pieces = [reach] * (own - 1) + [reach[:2] + [(6, 8), (8, 9)]]
    start(across)
    for a in range(own):
        for begin, end in pieces[a]:
            start(halo(a, begin, end))

    def apply_layer(stage, a, layer):
        src = fields[stage]
        at = layer + 9 - 3 * stage
        centre = src[a, at]
        result = diag[layer + 6] * centre
        for k in range(1, 4):
            near = src[a, at + k] + src[a, at - k]
            near = near + (pltpu.roll(centre, k, 0) + pltpu.roll(centre, ny - k, 0))
            near = near + (pltpu.roll(centre, k, 1) + pltpu.roll(centre, nz - k, 1))
            result = result + STEP[k] * near
        if stage > 0:
            result = 2.0 * result - fields[stage - 1][a, at + 3]
        if stage < 2:
            fields[stage + 1][a, at - 3] = result
        else:
            tiles = result.reshape(orbs, chunk, nz)
            slot = slot_layers.index(layer)
            third[:, a, slot] = tiles
            if slot < GATHERED:
                for q in range(2 * pairs - 1):
                    for parity in range(2):
                        spread[parity, q, a, slot] = tiles[2 * (q % pairs) + parity]

    inner = range(3, layers - 3)
    slot_layers = [*inner, 1, 2, layers - 3, layers - 2, 0, layers - 1]

    def newly(stage, a, begin, end):
        low, high = 3 * (stage + 1), layers - 3 * (stage + 1)
        for layer in (*range(low - end, low - begin), *range(high + begin, high + end)):
            apply_layer(stage, a, layer)

    slots_of = {(3, 6): ((0, half),), (6, 9): ((half, 6),), (6, 8): ((half, 4),), (8, 9): ((half + 4, 2),)}

    def to_cells(a, piece):
        part = pieces[a].index(piece) - 1
        for at, count in slots_of[piece]:

            @pl.loop(1, orbs)
            def _(p):
                to = lax.rem(o + 1 + lax.rem(p + 2, orbs - 1), orbs)
                pltpu.make_async_remote_copy(
                    src_ref=third.at[to, a, pl.ds(at, count)],
                    dst_ref=grouped.at[own * o + a, pl.ds(at, count)],
                    send_sem=fwd_send.at[a, part],
                    recv_sem=fwd_recv.at[a, part],
                    device_id={"orb": to},
                    device_id_type=MESH,
                ).start()

        for at, count in slots_of[piece]:
            for slot in range(at, at + count):
                grouped[own * o + a, slot] = third[o, a, slot]

    def wait_cells(a, part, sems):
        count = sum(count for _, count in slots_of[pieces[a][part + 1]])
        block = grouped.at[pl.ds(0, orbs - 1), pl.ds(0, count)]
        pltpu.make_async_copy(block, block, sems.at[a, part]).wait()

    def weigh(begin, end):
        @pl.loop(begin, end)
        def _(i):
            diag[i] = raw[i] * (1.0 / filter_half) + DIAGONAL

    wait(loads)
    weigh(6, layers + 6)
    for layer in inner:
        apply_layer(0, 0, layer)
    for copy in across:
        copy.wait()
    share_margins()
    for a in range(own):
        if a > 0:
            for layer in inner:
                apply_layer(0, a, layer)
        for begin, end in pieces[a]:
            wait(halo(a, begin, end))
            if a == 0 and begin == 3:
                wait_margins(pot_recv)
                weigh(0, 6)
                weigh(layers + 6, layers + 12)
            newly(0, a, begin, end)
            newly(1, a, begin, end)
            if begin > 0:
                newly(2, a, begin, end)
                to_cells(a, (begin, end))

    place, parity = o // 2, lax.rem(o, 2)
    other = o + 1 - 2 * parity

    def gather(a):
        @pl.loop(1, orbs)
        def _(p):
            to = lax.rem(o + 1 + lax.rem(p + 2, orbs - 1), orbs)
            pltpu.make_async_remote_copy(
                src_ref=spread.at[lax.rem(to, 2), pl.ds(to // 2 + 1, pairs - 1), a],
                dst_ref=wide.at[:, own * o + a],
                send_sem=all_send.at[0],
                recv_sem=all_recv.at[0],
                device_id={"orb": to},
                device_id_type=MESH,
            ).start()

    def gather_own():
        for k in range(1, pairs):
            for a in range(own):
                wide[k - 1, own * o + a] = spread[parity, place + k, a]

    def gather_rest():
        for a in range(own):
            gather(a)
        gather_own()

    def gather_wait(sem):
        block = wide.at[:, pl.ds(0, own * (orbs - 1))]
        pltpu.make_async_copy(block, block, sem.at[0]).wait()

    flat = grouped.reshape(n * layers * chunk, nz)
    flat_back = back.reshape(n * (layers - GATHERED) * chunk, nz)
    stride = layers * chunk

    def split_slots(ranges):
        def larger(slot, most):
            for r in range(chunk):
                most = jnp.maximum(most, jnp.abs(flat[pl.ds(slot * chunk + r, n, stride=stride), :]))
            return most

        most = jnp.zeros((n, nz), F32)
        for at, count in ranges:
            most = lax.fori_loop(at, at + count, larger, most, unroll=2)
        anchor = anchor_of(jnp.broadcast_to(jnp.max(most, axis=1, keepdims=True), (n, nz)))

        for at, count in ranges:

            @pl.loop(at, at + count, unroll=2)
            def _(slot):
                for r in range(chunk):
                    row = slot * chunk + r
                    x = flat[pl.ds(row, n, stride=stride), :]
                    lanes = pl.ds(pl.multiple_of(row * nz, nz), nz)
                    for part, value in enumerate(limbs(x, anchor)):
                        split_x[pl.ds(part * n, n), lanes] = value

    def gram_of(ranges, pair):
        for slot in (slot for at, count in ranges for slot in range(at, at + count)):
            x = split_x[:, slot * chunk * nz : (slot + 1) * chunk * nz]
            value = lax.dot_general(x, x, (((1,), (1,)), ((), ())), preferred_element_type=F32)
            if pair is None:
                pair = value, jnp.zeros_like(value)
            else:
                high, error = two_sum(pair[0], value)
                pair = high, pair[1] + error
        return pair

    lane = lax.broadcasted_iota(jnp.int32, (8, 128), 1)
    lane4 = lax.broadcasted_iota(jnp.int32, (4, 128), 1)
    lows = (lane4 & 32) == 32

    def total(pair):
        parts = [tuple(v[p * n : (p + 1) * n] for v in pair) for p in range(LIMBS)]
        low_first = add_pairs(add_pairs(parts[3], parts[2]), add_pairs(parts[1], parts[0]))
        pad = jnp.zeros((n, 128 - LIMBS * n), F32)
        wide = tuple(jnp.concatenate([v, pad], axis=1) for v in low_first)
        for step in (2 * n, n):
            wide = add_pairs(wide, tuple(pltpu.roll(v, 128 - step, 1) for v in wide))
        top, bottom = tuple(v[:8] for v in wide), tuple(pltpu.roll(v[8:], n, 1) for v in wide)
        high, low = (jnp.where(lane < n, t, b) for t, b in zip(top, bottom))
        packed = jnp.where(lane < 2 * n, high, pltpu.roll(low, 2 * n, 1))
        packed = jnp.where(lane4 < 64, packed[:4], pltpu.roll(packed, 64, 1)[4:])
        for which, (target, count, me, buf) in enumerate(
            ((near_device, near, place_near, gram_orb), (far_device, far, d // 2, gram_dom))
        ):
            buf[me] = packed

            @pl.loop(1, count)
            def _(p):
                pltpu.make_async_remote_copy(
                    src_ref=buf.at[me],
                    dst_ref=buf.at[me],
                    send_sem=gram_send.at[which],
                    recv_sem=gram_recv.at[which],
                    device_id=target(1 + lax.rem(p + count // 2 - 2, count - 1)),
                    device_id_type=MESH,
                ).start()

            if which == 0:
                gather_rest()
            block = buf.at[pl.ds(0, count - 1)]
            pltpu.make_async_copy(block, block, gram_recv.at[which]).wait()
            value, error = buf[...], None
            while count > 1:
                count //= 2
                value, extra = two_sum(value[:count], value[count:])
                error = extra if error is None else extra + (error[:count] + error[count:])
            packed = value[0] + jnp.where(lows, pltpu.roll(error[0], 2 * n, 1), 0.0)
        packed = jnp.concatenate([packed, pltpu.roll(packed, 64, 1)], axis=0)
        low = pltpu.roll(packed, 128 - 2 * n, 1)
        pair = tuple(
            jnp.where(
                lax.broadcasted_iota(jnp.int32, (n, 128), 1) < n,
                jnp.concatenate([v, pltpu.roll(v, 128 - n, 1)], axis=0),
                0.0,
            )
            for v in (packed, low)
        )
        return two_sum(pair[0], pair[1])

    def stacked(matrix):
        wide = matrix
        for part in range(1, LIMBS):
            wide = wide + pltpu.roll(matrix, part * n, 1)
        return jnp.concatenate(split3(wide), axis=0)[:, : LIMBS * n]

    def applied(weights, lanes):
        full = jnp.dot(weights, split_x[:, lanes], preferred_element_type=F32)
        return full[0:n] + (full[n : 2 * n] + full[2 * n : 3 * n])

    pair = None
    for part in range(3):
        for a in range(own):
            if part < len(pieces[a]) - 1:
                wait_cells(a, part, fwd_recv)
        ranges = slots_of[pieces[-1][part + 1]]
        split_slots(ranges)
        pair = gram_of(ranges, pair)
    gram = total(pair)
    matrix = combined(gram, float(cells), n)
    weights = stacked(matrix)

    parts = ((3 + GATHERED, layers - 3 - GATHERED, 0), (0, 3, layers - 3 - GATHERED))
    for part, (layer, count, at) in enumerate(parts):
        for i in range(count):
            slot = slot_layers.index(layer + i)
            y = applied(weights, pl.ds(slot * chunk * nz, chunk * nz))
            for r in range(chunk):
                flat_back[pl.ds((at + i) * chunk + r, n, stride=(layers - GATHERED) * chunk), :] = y[:, r * nz : (r + 1) * nz]

        @pl.loop(1, orbs)
        def _(p):
            to = lax.rem(o + 1 + lax.rem(p + 2, orbs - 1), orbs)
            pltpu.make_async_remote_copy(
                src_ref=back.at[pl.ds(own * to, own), pl.ds(at, count)],
                dst_ref=out_ref.at[:, pl.ds(layer, count), pl.ds(chunk * o, chunk)],
                send_sem=bck_send.at[part],
                recv_sem=bck_recv.at[part],
                device_id={"orb": to},
                device_id_type=MESH,
            ).start()

    all_rows = lax.broadcasted_iota(jnp.int32, (n, 128), 0)
    for i in range(2 * own):
        chosen = own * o + i if i < own else own * other + i - own
        row = jnp.sum(jnp.where(all_rows == chosen, matrix, 0.0), axis=0, keepdims=True)
        row = jnp.broadcast_to(row, (8, 128))
        for j in range(n):
            table[i, j] = lane_of(row, j)
    gather_wait(all_recv)

    def chunk_rows(k):
        return pl.ds(pl.multiple_of(chunk * (2 * lax.rem(place + k, pairs) + parity), chunk), chunk)

    @pl.loop(0, GATHERED)
    def _(slot):
        for k in range(pairs):
            x = [grouped[j, slot] if k == 0 else wide[k - 1, j, slot] for j in range(n)]
            for i in range(2 * own):
                terms = [table[i, j] * x[j] for j in range(n)]
                while len(terms) > 1:
                    terms = [p + q for p, q in zip(terms[::2], terms[1::2])]
                if i < own:
                    out_ref[i, slot + 3, chunk_rows(k), :] = terms[0]
                else:
                    swap[k, i - own, slot] = terms[0]

    for k in range(pairs):
        pltpu.make_async_remote_copy(
            src_ref=swap.at[k],
            dst_ref=out_ref.at[:, pl.ds(3, GATHERED), chunk_rows(k)],
            send_sem=swap_send.at[0],
            recv_sem=swap_recv.at[0],
            device_id={"orb": other},
            device_id_type=MESH,
        ).start()
    for a in range(own):
        for layer, count, at in parts:
            out_ref[a, pl.ds(layer, count), pl.ds(pl.multiple_of(chunk * o, chunk), chunk), :] = back[
                own * o + a, pl.ds(at, count)
            ]
    for sem in (swap_send, swap_recv):
        pltpu.make_async_copy(swap, swap, sem.at[0]).wait()
    for part, (_, count, at) in enumerate(parts):
        block = back.at[pl.ds(0, own * (orbs - 1)), pl.ds(at, count)]
        pltpu.make_async_copy(block, block, bck_send.at[part]).wait()
        pltpu.make_async_copy(block, block, bck_recv.at[part]).wait()
    gather_wait(all_send)
    wait_margins(pot_send)
    for a in range(own):
        for part in range(len(pieces[a]) - 1):
            wait_cells(a, part, fwd_send)
    for which, buf in enumerate((gram_orb, gram_dom)):
        block = buf.at[pl.ds(0, (near, far)[which] - 1)]
        pltpu.make_async_copy(block, block, gram_send.at[which]).wait()


def on_device(orbitals, potential):
    own, layers, ny, nz = orbitals.shape
    doms, orbs = lax.axis_size("dom"), lax.axis_size("orb")
    n = own * orbs
    chunk = ny // orbs
    cells = layers * doms * ny * nz
    width = layers * chunk * nz
    dma = pltpu.SemaphoreType.DMA

    def field(extra):
        return pltpu.VMEM((own, layers + extra, ny, nz), F32)

    return pl.pallas_call(
        functools.partial(kernel, (doms, orbs, own, layers, ny, nz, cells)),
        out_shape=pltpu.VMEM(orbitals.shape, F32),
        in_specs=[pl.BlockSpec(memory_space=pltpu.HBM)] * 2,
        out_specs=pl.BlockSpec(memory_space=pltpu.VMEM),
        scratch_shapes=[
            field(18),
            field(12),
            field(6),
            pltpu.VMEM((layers + 12, ny, nz), F32),
            pltpu.VMEM((layers + 12, ny, nz), F32),
            pltpu.VMEM((orbs, own, layers, chunk, nz), F32),
            pltpu.VMEM((2, orbs - 1, own, GATHERED, chunk, nz), F32),
            pltpu.VMEM((n, layers, chunk, nz), F32),
            pltpu.VMEM((orbs // 2 - 1, n, GATHERED, chunk, nz), F32),
            pltpu.VMEM((orbs // 2, own, GATHERED, chunk, nz), F32),
            pltpu.VMEM((2 * own, n, 8, 128), F32),
            pltpu.VMEM((LIMBS * n, width), BF16),
            pltpu.VMEM((n, layers - GATHERED, chunk, nz), F32),
            pltpu.VMEM((2 * orbs, 4, 128), F32),
            pltpu.VMEM((doms // 2, 4, 128), F32),
            dma((1 + own,)),
            dma((own, 4, 2)),
            dma((own, 4, 2)),
            dma((2, 2)),
            dma((2, 2)),
            dma((own, 3)),
            dma((own, 3)),
            dma((2,)),
            dma((2,)),
            dma((2,)),
            dma((2,)),
            dma((1,)),
            dma((1,)),
            dma((1,)),
            dma((1,)),
        ],
        compiler_params=pltpu.CompilerParams(
            collective_id=0, has_side_effects=True, vmem_limit_bytes=40 * 1024 * 1024
        ),
        cost_estimate=pl.CostEstimate(flops=100_000_000, bytes_accessed=4_000_000, transcendentals=0),
    )(*(pltpu.with_memory_space_constraint(v, pltpu.HBM) for v in (orbitals, potential)))


def solution(mesh):
    return jax.shard_map(
        on_device,
        mesh=mesh,
        in_specs=(P("orb", "dom", None, None), P("dom", None, None)),
        out_specs=P("orb", "dom", None, None),
        check_vma=False,
    )
```
